32 devices in a mesh: groups: 2 (over y), adapter: 4 (over z), mp: 2 (over x), kv: 2 (over core).
Axes of the slice: x: 2, y: 2, z: 4, core: 2. Of those that a mesh axis runs over, the one named last changes fastest.
Arguments:
- queries: bfloat16 [384, 8192], P(('groups', 'adapter'), 'mp'), parts along dimension 0
- keys: bfloat16 [384, 128, 1024], P(('groups', 'adapter'), 'kv', 'mp'), parts along dimension 0
- values: bfloat16 [384, 128, 1024], P(('groups', 'adapter'), 'kv', 'mp'), parts along dimension 0, may hold values from -6 to 6
- lengths: int32 [384], P(('groups', 'adapter')), parts along dimension 0, may hold values from 1 to 128, as said below
- row_adapter_index: int32 [384], P('groups'), parts along dimension 0, may hold values from 0 to 31, as said below
- residual: bfloat16 [384, 8192], P(('groups', 'mp'), ('adapter', 'kv')), parts along dimension 0, may hold values from -4 to 4
- output_weight: bfloat16 [8192, 8192], P('mp', ('adapter', 'kv')), may hold values from -0.0625 to 0.0625
- adapter_down_weight: bfloat16 [32, 8192, 64], P('adapter', ('mp', 'kv')), may hold values from -0.0625 to 0.0625
- adapter_up_weight: bfloat16 [32, 64, 8192], P('mp', None, ('adapter', 'kv')), may hold values from -0.75 to 0.75
Outputs:
- layer_out: bfloat16 [384, 8192], P(('groups', 'mp'), ('adapter', 'kv')), parts along dimension 0
The draws below stay inside these ranges and needn't reach their ends.
There are 2 independent parts, one for each index of `groups`. The reference program is written for one: setup_inputs(seed, part) draws one part's arguments, and reference() takes and returns one part's arrays. A program takes and returns all parts, laid end to end along the dimension named above; an argument that names none is the same for every part. Nothing has to cross between parts.
Inputs may be any that keep to these rules, and one draw needn't show every extreme that they name: `row_adapter_index`: among the 48 rows of each device (aligned blocks of the row order), the adapters of one owner (adapter // 8) are named by at most 24 rows, and by exactly 24 rows for some owner in every block. `lengths`: in every aligned block of 48 rows some row has 128 positions.
All inputs are finite; a program needn't handle non-finite values.
Results may differ from the reference program's by a relative error of at most 0.0053.
Values may be sent and summed in bfloat16 or wider, within the bound.
No kernel may reach another device: no remote copies, remote signals or barrier semaphores. Data moves between devices by JAX's collectives and lax.ppermute only.
A program may use at most 64 MiB of HBM per device.

```python
import math
import jax
import jax.numpy as jnp
from jax import lax

MODEL_WIDTH = 8192
H = 64
KVH = 8
HD = 128
ADAPTER_RANK = 64
ADP_DEV = 8
RPD = 48
L = 128
ADAPTER_POOL = 32
ROWS = 192
CAP = 24


def shared_cache(key):
    return jnp.clip(jax.random.normal(key, (ROWS, L, KVH * HD), jnp.float32), -6.0, 6.0)


def draw_keys(key, part):
    cached = shared_cache(key)
    return cached.astype(jnp.bfloat16)


def draw_queries(key, part):
    key = jax.random.fold_in(key, 12)
    entries = jnp.clip(jax.random.normal(key, (ROWS, H * HD), jnp.float32), -6.0, 6.0)
    return entries.astype(jnp.bfloat16)


def draw_lengths(key, part):
    key = jax.random.fold_in(key, 13)
    block_count = ROWS // RPD
    drawn = jax.random.randint(key, (ROWS,), 1, L + 1)
    longest = jax.random.randint(jax.random.fold_in(key, 1), (block_count,), 0, RPD)
    marked = jnp.arange(ROWS) % RPD == jnp.repeat(longest, RPD)
    return jnp.where(marked, L, drawn).astype(jnp.int32)


def draw_row_adapter_index(key, part):
    key = jax.random.fold_in(key, 14)
    block_count = ROWS // RPD
    slot_count = block_count * CAP

    def one_block(block_key):
        split_keys = jax.random.split(block_key, 4)
        ranking = jax.random.permutation(split_keys[0], slot_count)
        crowded = jax.random.randint(split_keys[1], (), 0, block_count)
        scores = jnp.where(jnp.arange(slot_count) // CAP == crowded, -1, ranking)
        picked = jnp.argsort(scores, stable=True)[:RPD]
        owners_of = picked // CAP
        owners_of = owners_of[jax.random.permutation(split_keys[2], RPD)]
        member = jax.random.randint(split_keys[3], (RPD,), 0, ADP_DEV)
        return owners_of * ADP_DEV + member
    return jax.vmap(one_block)(jax.random.split(key, block_count)).reshape(ROWS).astype(jnp.int32)


def levels(own_key, shape, cuts, low, high):
    factor_of, own = 1.0, jax.random.fold_in(own_key, 6)
    for axis_at, parts in cuts:
        draws = jnp.exp(jax.random.uniform(jax.random.fold_in(own, axis_at), (parts,), jnp.float32, low / len(cuts), high / len(cuts)))
        factor_of = factor_of * jnp.repeat(draws, shape[axis_at] // parts).reshape([-1 if axis == axis_at else 1 for axis in range(len(shape))])
    return factor_of


def gaussian(own_key, extent, deviation, most, shards=(), kind=jnp.bfloat16):
    result = jax.random.normal(own_key, extent, jnp.float32) * deviation
    if len(shards) > 0:
        result = levels(own_key, extent, shards, -0.22, 0.18) * result
    return jnp.clip(result, min=-most, max=most).astype(kind)


def setup_inputs(seed: int = 0, part: int = 0) -> dict:
    splits = jax.random.split(jax.random.key(seed), 10)
    own_keys = jax.random.split(jax.random.fold_in(splits[9], part), 10)
    queries = draw_queries(jax.random.fold_in(jax.random.fold_in(splits[9], part), 71), part)
    keys = draw_keys(jax.random.fold_in(jax.random.fold_in(splits[9], part), 71), part)
    values = gaussian(own_keys[2], (ROWS, L, KVH * HD), 1.0, 6.0, ((0, 4), (1, 2), (2, 2)))
    lengths = draw_lengths(jax.random.fold_in(jax.random.fold_in(splits[9], part), 71), part)
    row_adapter_index = draw_row_adapter_index(jax.random.fold_in(jax.random.fold_in(splits[9], part), 71), part)
    residual = gaussian(own_keys[5], (ROWS, MODEL_WIDTH), 0.25, 4.0, ((0, 2), (1, 8)))
    output_weight = gaussian(splits[6], (MODEL_WIDTH, MODEL_WIDTH), MODEL_WIDTH ** -0.5, 0.0625, ((0, 2), (1, 8)))
    adapter_down_weight = gaussian(splits[7], (ADAPTER_POOL, MODEL_WIDTH, ADAPTER_RANK), MODEL_WIDTH ** -0.5, 0.0625, ((0, 4), (1, 4)))
    adapter_up_weight = gaussian(splits[8], (ADAPTER_POOL, ADAPTER_RANK, MODEL_WIDTH), ADAPTER_RANK ** -0.5, 0.75, ((0, 2), (2, 8)))
    return dict(queries=queries, keys=keys, values=values, lengths=lengths, row_adapter_index=row_adapter_index, residual=residual, output_weight=output_weight, adapter_down_weight=adapter_down_weight, adapter_up_weight=adapter_up_weight)


def reference(queries, keys, values, lengths, row_adapter_index, residual, output_weight, adapter_down_weight, adapter_up_weight):
    group = H // KVH
    query_heads = queries.astype(jnp.float32).reshape(ROWS, KVH, group, HD)
    key_heads = keys.astype(jnp.float32).reshape(ROWS, L, KVH, HD)
    value_heads = values.astype(jnp.float32).reshape(ROWS, L, KVH, HD)
    scores = jnp.einsum('rgjd,rpgd->rgjp', query_heads, key_heads, precision=lax.Precision.HIGHEST) * (1.0 / math.sqrt(HD))
    valid = (jnp.arange(L, dtype=jnp.int32)[None, :] < lengths[:, None])[:, None, None, :]
    masked = jnp.where(valid, scores, jnp.float32(-1e+30))
    row_top = lax.optimization_barrier(jnp.max(masked, axis=3))
    weights = jnp.where(valid, jnp.exp(masked - row_top[..., None]), jnp.float32(0.0))
    weight_sum = lax.optimization_barrier(jnp.sum(weights, axis=3))
    weighted = jnp.einsum('rgjp,rpgd->rgjd', weights, value_heads, precision=lax.Precision.HIGHEST)
    attention_output = (weighted / weight_sum[..., None]).reshape(ROWS, MODEL_WIDTH).astype(jnp.bfloat16)
    base_product = jnp.dot(attention_output, output_weight, preferred_element_type=jnp.float32)

    def row_down_weight(pair):
        vector, lookup_index = pair
        weight_matrix = lax.dynamic_index_in_dim(adapter_down_weight, lookup_index, 0, keepdims=False)
        return jnp.dot(vector[None, :], weight_matrix, preferred_element_type=jnp.float32)[0]
    adapter_middle = lax.map(row_down_weight, (attention_output, row_adapter_index.astype(jnp.int32))).astype(jnp.bfloat16)

    def row_up_weight(pair):
        vector, lookup_index = pair
        weight_matrix = lax.dynamic_index_in_dim(adapter_up_weight, lookup_index, 0, keepdims=False)
        return jnp.dot(vector[None, :], weight_matrix, preferred_element_type=jnp.float32)[0]
    adapter_delta = 2.0 * lax.map(row_up_weight, (adapter_middle, row_adapter_index.astype(jnp.int32)))
    return (residual.astype(jnp.float32) + base_product + adapter_delta).astype(jnp.bfloat16)
```

```python
import functools
import math

import jax
import jax.numpy as jnp
from jax import lax
from jax.experimental import pallas as pl
from jax.experimental.pallas import tpu as pltpu
from jax.sharding import PartitionSpec as P

HD = 128
LANES = 128
MIB = 1 << 20

neg_big = -1e30
adapter_scale = 2.0
score_scale = 1.0 / math.sqrt(HD)
log2_e = 1.4426950408889634


vmem_spec = pl.BlockSpec(memory_space=pltpu.VMEM)


def whole(shape):
    return pl.BlockSpec(shape, lambda *_: (0,) * len(shape))


def attend_body(group, away, lengths, q_hbm, k_hbm, v_hbm, o_ref, s_ref, q_ref, k_ref, v_ref, sems):
    core = lax.axis_index("kv")
    half = 1 - core if away else core
    steps, positions = k_ref.shape[0], k_ref.shape[2]
    rows, features = q_ref.shape[1], q_ref.shape[2]
    kv_features = k_ref.shape[3]
    kv_heads = kv_features // HD
    offset = core * positions

    def copies(i):
        at = pl.ds(i * rows, rows)
        wide_at = pl.ds(pl.multiple_of(half * features, features), features)
        narrow_at = pl.ds(pl.multiple_of(half * kv_features, kv_features), kv_features)
        return (
            pltpu.make_async_copy(q_hbm.at[at, wide_at], q_ref.at[i], sems.at[0, i]),
            pltpu.make_async_copy(k_hbm.at[at, :, narrow_at], k_ref.at[i], sems.at[1, i]),
            pltpu.make_async_copy(v_hbm.at[at, :, narrow_at], v_ref.at[i], sems.at[2, i]),
        )

    for i in range(steps):
        for copy in copies(i):
            copy.start()

    wide = 8 * positions
    row_id = lax.broadcasted_iota(jnp.int32, (8, wide), 0)
    column = lax.broadcasted_iota(jnp.int32, (8, wide), 1)
    own_row = column // positions == row_id
    position = column % positions + offset
    lane = lax.broadcasted_iota(jnp.int32, (8, LANES), 1)
    ones = jnp.ones((wide, LANES), jnp.bfloat16)
    for i in range(steps):
        for copy in copies(i):
            copy.wait()
        queries = q_ref[i].astype(jnp.float32)
        outs = {}
        stats = []
        for sub in range(rows // 8):
            limit = jnp.zeros((8, wide), jnp.int32)
            for t in range(8):
                limit = jnp.where(row_id == t, lengths[i * rows + sub * 8 + t], limit)
            valid = own_row & (position < limit)
            stat = jnp.zeros((8, LANES), jnp.float32)
            for g in range(kv_heads):
                q = jnp.concatenate(
                    [
                        queries[sub * 8 : sub * 8 + 8, j * HD : (j + 1) * HD]
                        for j in range(g * group, (g + 1) * group)
                    ],
                    axis=0,
                ).astype(jnp.bfloat16)
                k = k_ref[i, sub * 8 : sub * 8 + 8, :, g * HD : (g + 1) * HD].reshape(wide, HD)
                v = v_ref[i, sub * 8 : sub * 8 + 8, :, g * HD : (g + 1) * HD].reshape(wide, HD)
                scores = lax.dot_general(
                    q, k, (((1,), (1,)), ((), ())), preferred_element_type=jnp.float32
                ).reshape(group, 8, wide)
                scores = jnp.where(valid[None], scores, neg_big)
                top = jnp.max(scores, axis=2, keepdims=True)
                weights = jnp.exp2((scores - top) * (score_scale * log2_e))
                weights = weights.astype(jnp.bfloat16).reshape(group * 8, wide)
                both = jnp.dot(
                    weights,
                    jnp.concatenate([v, ones], axis=1),
                    preferred_element_type=jnp.float32,
                )
                total = both[:, HD:]
                out = both[:, :HD] / total
                level = jnp.log2(total) + top.reshape(group * 8, 1) * (score_scale * log2_e)
                for j in range(group):
                    outs[sub, g * group + j] = out[j * 8 : j * 8 + 8]
                    stat = jnp.where(lane == g * group + j, level[j * 8 : j * 8 + 8], stat)
            stats.append(stat)
        at = slice(i * rows, (i + 1) * rows)
        for j in range(kv_heads * group):
            o_ref[at, j * HD : (j + 1) * HD] = jnp.concatenate(
                [outs[sub, j] for sub in range(rows // 8)], axis=0
            ).astype(o_ref.dtype)
        s_ref[at, :] = jnp.concatenate(stats, axis=0)


def attend(queries, keys, values, lengths, away, out_type):
    rows, features = queries.shape[0], queries.shape[1] // 2
    positions, kv_features = keys.shape[1], keys.shape[2] // 2
    block = 16
    steps = rows // block
    group = features // kv_features
    hbm = pl.BlockSpec(memory_space=pltpu.HBM)
    return pl.pallas_call(
        functools.partial(attend_body, group, away),
        in_specs=[pl.BlockSpec(memory_space=pltpu.SMEM), hbm, hbm, hbm],
        out_specs=[vmem_spec, vmem_spec],
        out_shape=[
            jax.ShapeDtypeStruct((rows, features), out_type),
            jax.ShapeDtypeStruct((rows, LANES), jnp.float32),
        ],
        scratch_shapes=[
            pltpu.VMEM((steps, block, features), jnp.bfloat16),
            pltpu.VMEM((steps, block, positions, kv_features), jnp.bfloat16),
            pltpu.VMEM((steps, block, positions, kv_features), jnp.bfloat16),
            pltpu.SemaphoreType.DMA((3, steps)),
        ],
        compiler_params=pltpu.CompilerParams(vmem_limit_bytes=12 * MIB),
        cost_estimate=pl.CostEstimate(
            flops=2_000_000_000, bytes_accessed=4_000_000, transcendentals=1_000_000
        ),
        name="attend",
    )(
        lengths,
        *(pltpu.with_memory_space_constraint(a, pltpu.HBM) for a in (queries, keys, values)),
    )


def merge_body(own_ref, own_level, other_ref, other_level, out_ref):
    share = 1.0 / (1.0 + jnp.exp2(own_level[...] - other_level[...]))
    for j in range(own_ref.shape[1] // HD):
        at = slice(j * HD, (j + 1) * HD)
        own = own_ref[:, at]
        other = other_ref[:, at].astype(jnp.float32)
        out_ref[:, at] = (own + (other - own) * share[:, j : j + 1]).astype(out_ref.dtype)


def merge(own, own_level, other, other_level):
    return pl.pallas_call(
        merge_body,
        out_shape=jax.ShapeDtypeStruct(own.shape, jnp.bfloat16),
        compiler_params=pltpu.CompilerParams(vmem_limit_bytes=8 * MIB),
        cost_estimate=pl.CostEstimate(
            flops=1_000_000, bytes_accessed=800_000, transcendentals=6_000
        ),
        name="merge",
    )(own, own_level, other, other_level)


def down_body(count, rank, ids_ref, d_ref, *refs):
    xs, out_ref = refs[:count], refs[count]
    picked_ref = refs[count + 1]
    me = lax.axis_index("adapter")
    rows = xs[0].shape[0]
    width = d_ref.shape[0]
    x = jnp.concatenate([r[...] for r in xs], axis=0) if count > 1 else xs[0][...]
    product = lax.dot_general(
        x, d_ref[...], (((1,), (1,)), ((), ())), preferred_element_type=jnp.float32
    )
    lane = lax.broadcasted_iota(jnp.int32, (rows, LANES), 1)
    per_tile = LANES // rank
    for j in range(count):
        source = lax.bitwise_xor(me, j) if count > 1 else 0
        at = pl.ds(pl.multiple_of(source * rows, 16), rows)
        member = ids_ref[at, :] - me * (width // rank)
        picked = jnp.zeros((rows, LANES), jnp.float32)
        for t in range(width // LANES):
            part = product[j * rows : (j + 1) * rows, t * LANES : (t + 1) * LANES]
            picked += jnp.where(member == t * per_tile + lane // rank, part, 0.0)
        picked_ref[at, :] = picked + pltpu.roll(picked, rank, 1)
    packed = out_ref.shape[0]
    left = lax.broadcasted_iota(jnp.int32, (packed, LANES), 1) < rank
    out_ref[...] = jnp.where(left, picked_ref[:packed, :], picked_ref[packed:, :])


def down(ids, weight, blocks):
    count, rows = len(blocks), len(blocks) * blocks[0].shape[0]
    rank = weight.shape[2]
    flat = jnp.transpose(weight, (0, 2, 1)).reshape(-1, weight.shape[1])
    return pl.pallas_call(
        functools.partial(down_body, count, rank),
        in_specs=[vmem_spec] * (2 + count),
        out_specs=vmem_spec,
        out_shape=jax.ShapeDtypeStruct((rows // 2, LANES), jnp.float32),
        scratch_shapes=[pltpu.VMEM((rows, LANES), jnp.float32)],
        compiler_params=pltpu.CompilerParams(vmem_limit_bytes=16 * MIB),
        cost_estimate=pl.CostEstimate(
            flops=2 * rows * flat.shape[0] * flat.shape[1],
            bytes_accessed=4_000_000,
            transcendentals=0,
        ),
        name="down",
    )(ids, flat, *blocks)


def up_body(count, rank, which, with_residual, ids_ref, base_ref, up_ref, *refs):
    mids, out_ref = refs[:count], refs[-1]
    side = lax.axis_index("mp")
    packed = mids[0][...]
    for r in mids[1:]:
        packed += r[...]
    packed = packed.astype(jnp.bfloat16).astype(jnp.float32)
    turned = pltpu.roll(packed, rank, 1)
    rows = out_ref.shape[0]
    left = lax.broadcasted_iota(jnp.int32, packed.shape, 1) < rank
    if which == "all":
        at = pl.ds(0, rows)
        total = jnp.concatenate(
            [jnp.where(left, packed, turned), jnp.where(left, turned, packed)], axis=0
        )
    else:
        part = side if which == "mine" else 1 - side
        at = pl.ds(pl.multiple_of(part * rows, 16), rows)
        total = jnp.where(left == (part == 0), packed, turned)
    lane = lax.broadcasted_iota(jnp.int32, (rows, LANES), 1)
    per_tile = LANES // rank
    local = ids_ref[at, :] - side * (up_ref.shape[0] // rank)
    spread = jnp.concatenate(
        [
            jnp.where(local == t * per_tile + lane // rank, total, 0.0)
            for t in range(up_ref.shape[0] // LANES)
        ],
        axis=1,
    ).astype(jnp.bfloat16)
    delta = jnp.dot(spread, up_ref[...], preferred_element_type=jnp.float32)
    out = base_ref[at, :] + adapter_scale * delta
    if with_residual:
        out += refs[count][...].astype(jnp.float32)
    out_ref[...] = out.astype(out_ref.dtype)


def up(ids, base, weight, mids, which, rows, residual, out_type):
    rank = weight.shape[1]
    flat = weight.reshape(-1, weight.shape[2])
    extra = [] if residual is None else [residual]
    return pl.pallas_call(
        functools.partial(up_body, len(mids), rank, which, residual is not None),
        in_specs=[vmem_spec] * (3 + len(mids) + len(extra)),
        out_specs=vmem_spec,
        out_shape=jax.ShapeDtypeStruct((rows, base.shape[1]), out_type),
        compiler_params=pltpu.CompilerParams(
            vmem_limit_bytes=(24 if which == "all" else 10) * MIB
        ),
        cost_estimate=pl.CostEstimate(
            flops=2 * rows * flat.shape[0] * flat.shape[1],
            bytes_accessed=3_000_000,
            transcendentals=0,
        ),
        name="up",
    )(ids, base, flat, *mids, *extra)


def last_body(kept_ref, back_ref, out_ref):
    out_ref[...] = (kept_ref[...] + back_ref[...].astype(jnp.float32)).astype(out_ref.dtype)


def last(kept, back):
    return pl.pallas_call(
        last_body,
        in_specs=[vmem_spec] * 2,
        out_specs=vmem_spec,
        out_shape=jax.ShapeDtypeStruct(kept.shape, jnp.bfloat16),
        compiler_params=pltpu.CompilerParams(vmem_limit_bytes=4 * MIB),
        name="last",
    )(kept, back)


def base_body(count, w_ref, *refs):
    xs, ys, out_ref = refs[:count], refs[count : 2 * count], refs[-1]
    me, half = lax.axis_index("adapter"), lax.axis_index("kv")
    rows, depth = xs[0].shape
    own = w_ref[pl.ds(pl.multiple_of(half * depth, depth), depth), :]
    other = w_ref[pl.ds(pl.multiple_of((1 - half) * depth, depth), depth), :]
    x = jnp.concatenate([r[...] for r in xs], axis=0) if count > 1 else xs[0][...]
    y = jnp.concatenate([r[...] for r in ys], axis=0) if count > 1 else ys[0][...]
    out = jnp.dot(x, own, preferred_element_type=jnp.float32)
    out += jnp.dot(y, other, preferred_element_type=jnp.float32)
    for j in range(count):
        source = lax.bitwise_xor(me, j) if count > 1 else 0
        at = pl.ds(pl.multiple_of(source * rows, 16), rows)
        out_ref[at, :] = out[j * rows : (j + 1) * rows]


def base_projection(weight, own, other):
    count = len(own)
    rows, depth = own[0].shape
    columns = weight.shape[1]
    tile = min(256, columns)
    return pl.pallas_call(
        functools.partial(base_body, count),
        grid=(columns // tile,),
        in_specs=[pl.BlockSpec((2 * depth, tile), lambda i: (0, i))]
        + [whole((rows, depth))] * (2 * count),
        out_specs=pl.BlockSpec((count * rows, tile), lambda i: (0, i)),
        out_shape=jax.ShapeDtypeStruct((count * rows, columns), jnp.float32),
        compiler_params=pltpu.CompilerParams(vmem_limit_bytes=24 * MIB),
        cost_estimate=pl.CostEstimate(
            flops=4 * count * rows * depth * columns,
            bytes_accessed=10_000_000,
            transcendentals=0,
        ),
        name="base",
    )(weight, *own, *other)


def swapped(x, axis, other=1):
    return lax.ppermute(x, axis, [(i, i ^ other) for i in range(lax.axis_size(axis))])


def local(
    queries,
    keys,
    values,
    lengths,
    row_adapter_index,
    residual,
    output_weight,
    adapter_down_weight,
    adapter_up_weight,
):
    owners, splits = lax.axis_size("adapter"), lax.axis_size("mp")
    entire_rows = row_adapter_index.shape[0]
    kept_rows = entire_rows // splits
    direct = owners == 4 and splits == 2
    ids = jnp.broadcast_to(row_adapter_index[:, None], (entire_rows, LANES))

    sent, sent_level = attend(queries, keys, values, lengths, True, jnp.float32)
    got, got_level = swapped(sent, "kv"), swapped(sent_level, "kv")
    own, own_level = attend(queries, keys, values, lengths, False, jnp.float32)
    attended = merge(own, own_level, got, got_level)

    if direct:
        blocks = [attended] + [swapped(attended, "adapter", j) for j in range(1, owners)]
    else:
        blocks = [lax.all_gather(attended, "adapter", axis=0, tiled=True)]
    others = [swapped(b, "kv") for b in blocks]
    part = down(ids, adapter_down_weight, blocks)
    base = base_projection(output_weight, blocks, others)

    if direct:
        part = part + swapped(part, "kv")
        part = part + swapped(part, "mp")
        mids = [part] + [swapped(part, "adapter", j) for j in range(1, owners)]
        away = up(
            ids, base, adapter_up_weight, mids, "theirs", kept_rows, None, jnp.bfloat16
        )
        back = swapped(away, "mp")
        kept = up(
            ids, base, adapter_up_weight, mids, "mine", kept_rows, residual, jnp.float32
        )
        return last(kept, back)
    mids = [lax.psum(part, ("adapter", "mp", "kv"))]
    terms = up(ids, base, adapter_up_weight, mids, "all", entire_rows, None, jnp.float32)
    summed = lax.psum_scatter(terms, "mp", scatter_dimension=0, tiled=True)
    return (residual.astype(jnp.float32) + summed).astype(jnp.bfloat16)


def solution(mesh):
    placed = (
        P(("groups", "adapter"), "mp"),
        P(("groups", "adapter"), "kv", "mp"),
        P(("groups", "adapter"), "kv", "mp"),
        P(("groups", "adapter")),
        P("groups"),
        P(("groups", "mp"), ("adapter", "kv")),
        P("mp", ("adapter", "kv")),
        P("adapter", ("mp", "kv"), None),
        P("mp", None, ("adapter", "kv")),
    )
    return jax.shard_map(
        local,
        mesh=mesh,
        in_specs=placed,
        out_specs=P(("groups", "mp"), ("adapter", "kv")),
        check_vma=False,
    )
```

```python
import functools
import math

import jax
import jax.numpy as jnp
from jax import lax
from jax.experimental import pallas as pl
from jax.experimental.pallas import tpu as pltpu
from jax.sharding import PartitionSpec as P

HD = 128
LANES = 128
MIB = 1 << 20

neg_big = -1e30
adapter_scale = 2.0
score_scale = 1.0 / math.sqrt(HD)
log2_e = 1.4426950408889634


vmem_spec = pl.BlockSpec(memory_space=pltpu.VMEM)
light = pl.CostEstimate(flops=1000, bytes_accessed=1000, transcendentals=0)


def attend_away_body(group, lengths_hbm, q_hbm, k_hbm, v_hbm, o_ref, s_ref, *refs):
    own, fetched, (lengths, sems, sem) = refs[:3], refs[3:6], refs[6:]
    core = lax.axis_index("kv")
    steps, rows = own[0].shape[:2]

    def copies(half, dst, first, i):
        at = pl.ds(i * rows, rows)
        for n, (hbm, ref) in enumerate(zip((q_hbm, k_hbm, v_hbm), dst)):
            width = ref.shape[-1]
            columns = pl.ds(pl.multiple_of(half * width, width), width)
            src = hbm.at[at, columns] if n == 0 else hbm.at[at, :, columns]
            yield pltpu.make_async_copy(src, ref.at[i], sems.at[first + n, i])

    number = pltpu.make_async_copy(lengths_hbm, lengths, sem)
    number.start()
    for half, dst, first in ((1 - core, fetched, 0), (core, own, 3)):
        for i in range(steps):
            for copy in copies(half, dst, first, i):
                copy.start()
    number.wait()
    for i in range(steps):
        for copy in copies(1 - core, fetched, 0, i):
            copy.wait()
        attend_block(group, core, i, lengths, *fetched, o_ref, s_ref)
    for i in range(steps):
        for copy in copies(core, own, 3, i):
            copy.wait()


def attend_own_body(group, lengths, q_ref, k_ref, v_ref, o_ref, s_ref):
    for i in range(q_ref.shape[0]):
        attend_block(group, lax.axis_index("kv"), i, lengths, q_ref, k_ref, v_ref, o_ref, s_ref)


def attend_block(group, core, i, lengths, q_ref, k_ref, v_ref, o_ref, s_ref):
    positions = k_ref.shape[2]
    rows, kv_heads = q_ref.shape[1], k_ref.shape[3] // HD
    offset = core * positions
    wide = 8 * positions
    row_id = lax.broadcasted_iota(jnp.int32, (8, wide), 0)
    column = lax.broadcasted_iota(jnp.int32, (8, wide), 1)
    own_row = column // positions == row_id
    position = column % positions + offset
    lane = lax.broadcasted_iota(jnp.int32, (8, LANES), 1)
    ones = jnp.ones((wide, LANES), jnp.bfloat16)
    queries = q_ref[i].astype(jnp.float32)
    outs = {}
    stats = []
    for sub in range(rows // 8):
        limit = jnp.zeros((8, wide), jnp.int32)
        for t in range(8):
            limit = jnp.where(row_id == t, lengths[i * rows + sub * 8 + t], limit)
        valid = own_row & (position < limit)
        stat = jnp.zeros((8, LANES), jnp.float32)
        for g in range(kv_heads):
            q = jnp.concatenate(
                [
                    queries[sub * 8 : sub * 8 + 8, j * HD : (j + 1) * HD]
                    for j in range(g * group, (g + 1) * group)
                ],
                axis=0,
            ).astype(jnp.bfloat16)
            k = k_ref[i, sub * 8 : sub * 8 + 8, :, g * HD : (g + 1) * HD].reshape(wide, HD)
            v = v_ref[i, sub * 8 : sub * 8 + 8, :, g * HD : (g + 1) * HD].reshape(wide, HD)
            scores = lax.dot_general(
                q, k, (((1,), (1,)), ((), ())), preferred_element_type=jnp.float32
            ).reshape(group, 8, wide)
            scores = jnp.where(valid[None], scores, neg_big)
            top = jnp.max(scores, axis=2, keepdims=True)
            weights = jnp.exp2((scores - top) * (score_scale * log2_e))
            weights = weights.astype(jnp.bfloat16).reshape(group * 8, wide)
            both = jnp.dot(
                weights,
                jnp.concatenate([v, ones], axis=1),
                preferred_element_type=jnp.float32,
            )
            total = both[:, HD:]
            out = both[:, :HD] / total
            level = jnp.log2(total) + top.reshape(group * 8, 1) * (score_scale * log2_e)
            for j in range(group):
                outs[sub, g * group + j] = out[j * 8 : j * 8 + 8]
                stat = jnp.where(lane == g * group + j, level[j * 8 : j * 8 + 8], stat)
        stats.append(stat)
    at = slice(i * rows, (i + 1) * rows)
    for j in range(kv_heads * group):
        o_ref[at, j * HD : (j + 1) * HD] = jnp.concatenate(
            [outs[sub, j] for sub in range(rows // 8)], axis=0
        ).astype(o_ref.dtype)
    s_ref[at, :] = jnp.concatenate(stats, axis=0)


def attend_away(queries, keys, values, lengths):
    rows, features = queries.shape[0], queries.shape[1] // 2
    positions, kv_features = keys.shape[1], keys.shape[2] // 2
    block = 16
    steps = rows // block
    hbm = pl.BlockSpec(memory_space=pltpu.HBM)
    pieces = [
        (steps, block, features),
        (steps, block, positions, kv_features),
        (steps, block, positions, kv_features),
    ]
    return pl.pallas_call(
        functools.partial(attend_away_body, features // kv_features),
        in_specs=[hbm] * 4,
        out_specs=[vmem_spec] * 5,
        out_shape=[
            jax.ShapeDtypeStruct((rows, features), jnp.float32),
            jax.ShapeDtypeStruct((rows, LANES), jnp.float32),
        ]
        + [jax.ShapeDtypeStruct(shape, jnp.bfloat16) for shape in pieces],
        scratch_shapes=[pltpu.VMEM(shape, jnp.bfloat16) for shape in pieces]
        + [
            pltpu.SMEM((rows,), jnp.int32),
            pltpu.SemaphoreType.DMA((6, steps)),
            pltpu.SemaphoreType.DMA,
        ],
        compiler_params=pltpu.CompilerParams(vmem_limit_bytes=16 * MIB),
        cost_estimate=light,
        name="attend_away",
    )(
        *(
            pltpu.with_memory_space_constraint(a, pltpu.HBM)
            for a in (lengths, queries, keys, values)
        )
    )


def attend_own(queries, keys, values, lengths):
    steps, block, features = queries.shape
    group = features // keys.shape[3]
    return pl.pallas_call(
        functools.partial(attend_own_body, group),
        in_specs=[pl.BlockSpec(memory_space=pltpu.SMEM)] + [vmem_spec] * 3,
        out_specs=[vmem_spec] * 2,
        out_shape=[
            jax.ShapeDtypeStruct((steps * block, features), jnp.float32),
            jax.ShapeDtypeStruct((steps * block, LANES), jnp.float32),
        ],
        compiler_params=pltpu.CompilerParams(vmem_limit_bytes=12 * MIB),
        cost_estimate=light,
        name="attend_own",
    )(lengths, queries, keys, values)


def places(ids, target, owned_count):
    rows = ids.shape[0]
    member = ids - target * owned_count
    owned = (member >= 0) & (member < owned_count)
    mark = jnp.where(owned, 1.0, 0.0)
    earlier = lax.broadcasted_iota(jnp.int32, (rows, rows), 1) < lax.broadcasted_iota(
        jnp.int32, (rows, rows), 0
    )
    before = jnp.dot(
        jnp.where(earlier, 1.0, 0.0).astype(jnp.bfloat16),
        mark.astype(jnp.bfloat16),
        preferred_element_type=jnp.float32,
    )
    count = jnp.sum(mark, axis=0, keepdims=True)
    row = lax.broadcasted_iota(jnp.int32, ids.shape, 0).astype(jnp.float32)
    return jnp.where(owned, before, count + row - before)


def merge_body(owned_count, own_ref, own_level, other_ref, other_level, ids_ref, out_ref, *fronts):
    rows = own_ref.shape[0]
    share = 1.0 / (1.0 + jnp.exp2(own_level[...] - other_level[...]))
    for j in range(own_ref.shape[1] // HD):
        at = slice(j * HD, (j + 1) * HD)
        own = own_ref[:, at]
        other = other_ref[:, at].astype(jnp.float32)
        out_ref[:, at] = (own + (other - own) * share[:, j : j + 1]).astype(out_ref.dtype)
    for j, ref in enumerate(fronts):
        route_to(j + 1, owned_count, ids_ref, out_ref, ref, 0)


def route_to(shift, owned_count, ids_ref, rows_ref, out_ref, first):
    rows, slots = rows_ref.shape[0], out_ref.shape[0]
    me = lax.axis_index("adapter")
    ids = ids_ref[pl.ds(pl.multiple_of(me * rows, 16), rows), :]
    place = places(ids, lax.bitwise_xor(me, shift), owned_count).T
    slot = lax.broadcasted_iota(jnp.int32, (slots, rows), 0) + first
    take = jnp.where(place[:slots, :] == slot.astype(jnp.float32), 1.0, 0.0)
    out_ref[...] = jnp.dot(
        take.astype(jnp.bfloat16), rows_ref[...], preferred_element_type=jnp.float32
    ).astype(out_ref.dtype)


def merge(own, own_level, other, other_level, ids, owned_count, partners, capacity):
    shapes = [own.shape] + [(capacity, own.shape[1])] * partners
    return pl.pallas_call(
        functools.partial(merge_body, owned_count),
        in_specs=[vmem_spec] * 5,
        out_specs=[vmem_spec] * len(shapes),
        out_shape=[jax.ShapeDtypeStruct(s, jnp.bfloat16) for s in shapes],
        compiler_params=pltpu.CompilerParams(vmem_limit_bytes=10 * MIB),
        cost_estimate=light,
        name="merge",
    )(own, own_level, other, other_level, ids)


def route_rest_body(first, owned_count, ids_ref, rows_ref, _, *outs):
    for j, ref in enumerate(outs):
        route_to(j + 1, owned_count, ids_ref, rows_ref, ref, first)


def route_rest(ids, rows, after, first, owned_count, partners):
    shape = (rows.shape[0] - first, rows.shape[1])
    return pl.pallas_call(
        functools.partial(route_rest_body, first, owned_count),
        in_specs=[vmem_spec] * 2 + [pl.BlockSpec(memory_space=pl.ANY)],
        out_specs=[vmem_spec] * partners,
        out_shape=[jax.ShapeDtypeStruct(shape, jnp.bfloat16)] * partners,
        compiler_params=pltpu.CompilerParams(vmem_limit_bytes=6 * MIB),
        cost_estimate=light,
        name="route_rest",
    )(ids, rows, after)


def put_back(ids, source, part, first, owned_count):
    rows, slots = ids.shape[0], part.shape[0]
    me = lax.axis_index("adapter")
    place = places(ids, me, owned_count)
    slot = lax.broadcasted_iota(jnp.int32, (rows, slots), 1) + first
    put = jnp.where(place[:, :slots] == slot.astype(jnp.float32), 1.0, 0.0)
    return jnp.dot(put.astype(jnp.bfloat16), part, preferred_element_type=jnp.float32)


def restore_body(count, owned_count, ids_ref, *refs):
    fronts, backs, out_ref = refs[:count], refs[count : 2 * count], refs[-1]
    rows = out_ref.shape[0] // count
    for j in range(count):
        source = lax.bitwise_xor(lax.axis_index("adapter"), j + 1)
        ids = ids_ref[pl.ds(pl.multiple_of(source * rows, 16), rows), :]
        front = put_back(ids, source, fronts[j][...], 0, owned_count)
        back = put_back(ids, source, backs[j][...], fronts[j].shape[0], owned_count)
        out_ref[j * rows : (j + 1) * rows, :] = (front + back).astype(out_ref.dtype)


def restore(ids, fronts, backs, after, owned_count):
    count = len(fronts)
    rows, features = fronts[0].shape[0] + backs[0].shape[0], fronts[0].shape[1]
    return pl.pallas_call(
        functools.partial(restore_body, count, owned_count),
        in_specs=[vmem_spec] * (1 + 2 * count) + [pl.BlockSpec(memory_space=pl.ANY)],
        out_specs=vmem_spec,
        out_shape=jax.ShapeDtypeStruct((count * rows, features), jnp.bfloat16),
        compiler_params=pltpu.CompilerParams(vmem_limit_bytes=8 * MIB),
        cost_estimate=light,
        name="restore",
    )(ids, *fronts, *backs, after)


def down_body(count, rank, ids_ref, d_ref, *refs):
    xs, (out_ref, picked_ref) = refs[:count], refs[-2:]
    me = lax.axis_index("adapter")
    rows = xs[0].shape[0]
    width = d_ref.shape[0]
    parts = [xs[0][...]]
    for j in range(1, count):
        source = lax.bitwise_xor(me, j)
        ids = ids_ref[pl.ds(pl.multiple_of(source * rows, 16), rows), :]
        parts.append(put_back(ids, source, xs[j][...], 0, width // rank).astype(jnp.bfloat16))
    x = jnp.concatenate(parts, axis=0) if count > 1 else parts[0]
    product = lax.dot_general(
        x, d_ref[...], (((1,), (1,)), ((), ())), preferred_element_type=jnp.float32
    )
    lane = lax.broadcasted_iota(jnp.int32, (rows, LANES), 1)
    per_tile = LANES // rank
    for j in range(count):
        source = lax.bitwise_xor(me, j) if count > 1 else 0
        at = pl.ds(pl.multiple_of(source * rows, 16), rows)
        member = ids_ref[at, :] - me * (width // rank)
        picked = jnp.zeros((rows, LANES), jnp.float32)
        for t in range(width // LANES):
            part = product[j * rows : (j + 1) * rows, t * LANES : (t + 1) * LANES]
            picked += jnp.where(member == t * per_tile + lane // rank, part, 0.0)
        picked_ref[at, :] = picked + pltpu.roll(picked, rank, 1)
    packed = out_ref.shape[0]
    left = lax.broadcasted_iota(jnp.int32, (packed, LANES), 1) < rank
    out_ref[...] = jnp.where(left, picked_ref[:packed, :], picked_ref[packed:, :])


def down(ids, weight, blocks, after=()):
    count, rows = len(blocks), len(blocks) * blocks[0].shape[0]
    rank = weight.shape[2]
    flat = jnp.transpose(weight, (0, 2, 1)).reshape(-1, weight.shape[1])
    return pl.pallas_call(
        functools.partial(down_body, count, rank),
        in_specs=[vmem_spec] * (2 + count) + [pl.BlockSpec(memory_space=pl.ANY)] * len(after),
        out_specs=vmem_spec,
        out_shape=jax.ShapeDtypeStruct((rows // 2, LANES), jnp.float32),
        scratch_shapes=[pltpu.VMEM((rows, LANES), jnp.float32)],
        compiler_params=pltpu.CompilerParams(vmem_limit_bytes=16 * MIB),
        cost_estimate=light,
        name="down",
    )(ids, flat, *blocks, *after)


def up_body(count, rank, which, with_residual, ids_ref, base_ref, up_ref, *refs):
    mids, out_ref = refs[:count], refs[-1]
    side = lax.axis_index("mp")
    packed = mids[0][...]
    for r in mids[1:]:
        packed += r[...]
    packed = packed.astype(jnp.bfloat16).astype(jnp.float32)
    turned = pltpu.roll(packed, rank, 1)
    rows = out_ref.shape[0]
    left = lax.broadcasted_iota(jnp.int32, packed.shape, 1) < rank
    if which == "all":
        at = pl.ds(0, rows)
        total = jnp.concatenate(
            [jnp.where(left, packed, turned), jnp.where(left, turned, packed)], axis=0
        )
    else:
        part = side if which == "mine" else 1 - side
        at = pl.ds(pl.multiple_of(part * rows, 16), rows)
        total = jnp.where(left == (part == 0), packed, turned)
    lane = lax.broadcasted_iota(jnp.int32, (rows, LANES), 1)
    per_tile = LANES // rank
    local = ids_ref[at, :] - side * (up_ref.shape[0] // rank)
    spread = jnp.concatenate(
        [
            jnp.where(local == t * per_tile + lane // rank, total, 0.0)
            for t in range(up_ref.shape[0] // LANES)
        ],
        axis=1,
    ).astype(jnp.bfloat16)
    delta = jnp.dot(spread, up_ref[...], preferred_element_type=jnp.float32)
    out = base_ref[at, :] + adapter_scale * delta
    if with_residual:
        out += refs[count][...].astype(jnp.float32)
    out_ref[...] = out.astype(out_ref.dtype)


def up(ids, base, weight, mids, which, rows, residual, out_type):
    rank = weight.shape[1]
    flat = weight.reshape(-1, weight.shape[2])
    extra = [] if residual is None else [residual]
    return pl.pallas_call(
        functools.partial(up_body, len(mids), rank, which, residual is not None),
        in_specs=[vmem_spec] * (3 + len(mids) + len(extra)),
        out_specs=vmem_spec,
        out_shape=jax.ShapeDtypeStruct((rows, base.shape[1]), out_type),
        compiler_params=pltpu.CompilerParams(
            vmem_limit_bytes=(24 if which == "all" else 10) * MIB
        ),
        cost_estimate=light,
        name="up",
    )(ids, base, flat, *mids, *extra)


def last_body(kept_ref, back_ref, out_ref):
    out_ref[...] = (kept_ref[...] + back_ref[...].astype(jnp.float32)).astype(out_ref.dtype)


def last(kept, back):
    return pl.pallas_call(
        last_body,
        in_specs=[vmem_spec] * 2,
        out_specs=vmem_spec,
        out_shape=jax.ShapeDtypeStruct(kept.shape, jnp.bfloat16),
        compiler_params=pltpu.CompilerParams(vmem_limit_bytes=4 * MIB),
        name="last",
    )(kept, back)


def base_body(count, unit, tile, w_ref, *refs):
    xs, ys, out_ref = refs[:count], refs[count : 2 * count], refs[-1]
    me, half = lax.axis_index("adapter"), lax.axis_index("kv")
    depth = xs[0].shape[1]
    x = jnp.concatenate([r[...] for r in xs], axis=0) if count > 1 else xs[0][...]
    y = jnp.concatenate([r[...] for r in ys], axis=0) if count > 1 else ys[0][...]
    own = pl.ds(pl.multiple_of(half * depth, depth), depth)
    other = pl.ds(pl.multiple_of((1 - half) * depth, depth), depth)
    for t in range(out_ref.shape[1] // tile):
        at = slice(t * tile, (t + 1) * tile)
        out = jnp.dot(x, w_ref[own, at], preferred_element_type=jnp.float32)
        out += jnp.dot(y, w_ref[other, at], preferred_element_type=jnp.float32)
        for j in range(out.shape[0] // unit):
            source = lax.bitwise_xor(me, j) if count > 1 else 0
            block = pl.ds(pl.multiple_of(source * unit, 16), unit)
            out_ref[block, at] = out[j * unit : (j + 1) * unit]


def base_projection(weight, own, other):
    count = len(own)
    rows = sum(b.shape[0] for b in own)
    columns = weight.shape[1]
    unit = own[0].shape[0]
    return pl.pallas_call(
        functools.partial(base_body, count, unit, min(256, columns)),
        in_specs=[vmem_spec] * (1 + 2 * count),
        out_specs=vmem_spec,
        out_shape=jax.ShapeDtypeStruct((rows, columns), jnp.float32),
        compiler_params=pltpu.CompilerParams(vmem_limit_bytes=24 * MIB),
        cost_estimate=light,
        name="base",
    )(weight, *own, *other)


def swapped(x, axis, other=1):
    return lax.ppermute(x, axis, [(i, i ^ other) for i in range(lax.axis_size(axis))])


def local(
    queries,
    keys,
    values,
    lengths,
    row_adapter_index,
    residual,
    output_weight,
    adapter_down_weight,
    adapter_up_weight,
):
    owners, splits = lax.axis_size("adapter"), lax.axis_size("mp")
    entire_rows = row_adapter_index.shape[0]
    kept_rows = entire_rows // splits
    direct = owners == 4 and splits == 2
    owned_count = adapter_down_weight.shape[0]
    capacity = 2 * queries.shape[0] // owners
    ids = jnp.broadcast_to(row_adapter_index[:, None], (entire_rows, LANES))

    sent, sent_level, *own_operands = attend_away(queries, keys, values, lengths)
    got, got_level = swapped(sent, "kv"), swapped(sent_level, "kv")
    own, own_level = attend_own(*own_operands, lengths)
    partners = range(1, owners) if direct else ()
    attended, *fronts = merge(
        own, own_level, got, got_level, ids, owned_count, len(partners), capacity
    )

    if direct:
        fronts = [swapped(f, "adapter", j) for j, f in zip(partners, fronts)]
        backs = route_rest(ids, attended, fronts[0], capacity, owned_count, len(partners))
        part = down(ids, adapter_down_weight, [attended] + fronts, backs[:1])
        backs = [swapped(b, "adapter", j) for j, b in zip(partners, backs)]
        far = swapped(part, "mp")
        part = part + far
        part = part + swapped(part, "kv")
        blocks = [attended, restore(ids, fronts, backs, far, owned_count)]
    else:
        blocks = [lax.all_gather(attended, "adapter", axis=0, tiled=True)]
        part = down(ids, adapter_down_weight, blocks)
    others = [swapped(b, "kv") for b in blocks]
    base = base_projection(output_weight, blocks, others)

    if direct:
        mids = [part] + [swapped(part, "adapter", j) for j in range(1, owners)]
        away = up(
            ids, base, adapter_up_weight, mids, "theirs", kept_rows, None, jnp.bfloat16
        )
        back = swapped(away, "mp")
        kept = up(
            ids, base, adapter_up_weight, mids, "mine", kept_rows, residual, jnp.float32
        )
        return last(kept, back)
    mids = [lax.psum(part, ("adapter", "mp", "kv"))]
    terms = up(ids, base, adapter_up_weight, mids, "all", entire_rows, None, jnp.float32)
    summed = lax.psum_scatter(terms, "mp", scatter_dimension=0, tiled=True)
    return (residual.astype(jnp.float32) + summed).astype(jnp.bfloat16)


def solution(mesh):
    placed = (
        P(("groups", "adapter"), "mp"),
        P(("groups", "adapter"), "kv", "mp"),
        P(("groups", "adapter"), "kv", "mp"),
        P(("groups", "adapter")),
        P("groups"),
        P(("groups", "mp"), ("adapter", "kv")),
        P("mp", ("adapter", "kv")),
        P("adapter", ("mp", "kv"), None),
        P("mp", None, ("adapter", "kv")),
    )
    return jax.shard_map(
        local,
        mesh=mesh,
        in_specs=placed,
        out_specs=P(("groups", "mp"), ("adapter", "kv")),
        check_vma=False,
    )
```

```python
import functools
import math

import jax
import jax.numpy as jnp
from jax import lax
from jax.experimental import pallas as pl
from jax.experimental.pallas import tpu as pltpu
from jax.sharding import PartitionSpec as P

HD = 128
LANES = 128
MIB = 1 << 20

neg_big = -1e30
adapter_scale = 2.0
score_scale = 1.0 / math.sqrt(HD)
log2_e = 1.4426950408889634


vmem_spec = pl.BlockSpec(memory_space=pltpu.VMEM)
light = pl.CostEstimate(flops=1000, bytes_accessed=1000, transcendentals=0)


def attend_away_body(group, lengths_hbm, q_hbm, k_hbm, v_hbm, o_ref, s_ref, *refs):
    own, fetched, (lengths, sems, sem) = refs[:3], refs[3:6], refs[6:]
    core = lax.axis_index("kv")
    steps, rows = own[0].shape[:2]

    def copies(half, dst, first, i):
        at = pl.ds(i * rows, rows)
        for n, (hbm, ref) in enumerate(zip((q_hbm, k_hbm, v_hbm), dst)):
            width = ref.shape[-1]
            columns = pl.ds(pl.multiple_of(half * width, width), width)
            src = hbm.at[at, columns] if n == 0 else hbm.at[at, :, columns]
            yield pltpu.make_async_copy(src, ref.at[i], sems.at[first + n, i])

    number = pltpu.make_async_copy(lengths_hbm, lengths, sem)
    number.start()
    for half, dst, first in ((1 - core, fetched, 0), (core, own, 3)):
        for i in range(steps):
            for copy in copies(half, dst, first, i):
                copy.start()
    number.wait()
    for i in range(steps):
        for copy in copies(1 - core, fetched, 0, i):
            copy.wait()
        attend_block(group, core, i, lengths, *fetched, o_ref, s_ref)
    for i in range(steps):
        for copy in copies(core, own, 3, i):
            copy.wait()


def attend_own_body(group, lengths, q_ref, k_ref, v_ref, o_ref, s_ref):
    for i in range(q_ref.shape[0]):
        attend_block(group, lax.axis_index("kv"), i, lengths, q_ref, k_ref, v_ref, o_ref, s_ref)


def attend_block(group, core, i, lengths, q_ref, k_ref, v_ref, o_ref, s_ref):
    positions = k_ref.shape[2]
    rows, kv_heads = q_ref.shape[1], k_ref.shape[3] // HD
    offset = core * positions
    wide = 8 * positions
    row_id = lax.broadcasted_iota(jnp.int32, (8, wide), 0)
    column = lax.broadcasted_iota(jnp.int32, (8, wide), 1)
    own_row = column // positions == row_id
    position = column % positions + offset
    lane = lax.broadcasted_iota(jnp.int32, (8, LANES), 1)
    ones = jnp.ones((wide, LANES), jnp.bfloat16)
    queries = q_ref[i].astype(jnp.float32)
    outs = {}
    stats = []
    for sub in range(rows // 8):
        limit = jnp.zeros((8, wide), jnp.int32)
        for t in range(8):
            limit = jnp.where(row_id == t, lengths[i * rows + sub * 8 + t], limit)
        valid = own_row & (position < limit)
        stat = jnp.zeros((8, LANES), jnp.float32)
        for g in range(kv_heads):
            q = jnp.concatenate(
                [
                    queries[sub * 8 : sub * 8 + 8, j * HD : (j + 1) * HD]
                    for j in range(g * group, (g + 1) * group)
                ],
                axis=0,
            ).astype(jnp.bfloat16)
            k = k_ref[i, sub * 8 : sub * 8 + 8, :, g * HD : (g + 1) * HD].reshape(wide, HD)
            v = v_ref[i, sub * 8 : sub * 8 + 8, :, g * HD : (g + 1) * HD].reshape(wide, HD)
            scores = lax.dot_general(
                q, k, (((1,), (1,)), ((), ())), preferred_element_type=jnp.float32
            ).reshape(group, 8, wide)
            scores = jnp.where(valid[None], scores, neg_big)
            top = jnp.max(scores, axis=2, keepdims=True)
            weights = jnp.exp2((scores - top) * (score_scale * log2_e))
            weights = weights.astype(jnp.bfloat16).reshape(group * 8, wide)
            both = jnp.dot(
                weights,
                jnp.concatenate([v, ones], axis=1),
                preferred_element_type=jnp.float32,
            )
            total = both[:, HD:]
            out = both[:, :HD] / total
            level = jnp.log2(total) + top.reshape(group * 8, 1) * (score_scale * log2_e)
            for j in range(group):
                outs[sub, g * group + j] = out[j * 8 : j * 8 + 8]
                stat = jnp.where(lane == g * group + j, level[j * 8 : j * 8 + 8], stat)
        stats.append(stat)
    at = slice(i * rows, (i + 1) * rows)
    for j in range(kv_heads * group):
        o_ref[at, j * HD : (j + 1) * HD] = jnp.concatenate(
            [outs[sub, j] for sub in range(rows // 8)], axis=0
        ).astype(o_ref.dtype)
    s_ref[at, :] = jnp.concatenate(stats, axis=0)


def attend_away(queries, keys, values, lengths):
    rows, features = queries.shape[0], queries.shape[1] // 2
    positions, kv_features = keys.shape[1], keys.shape[2] // 2
    block = 16
    steps = rows // block
    hbm = pl.BlockSpec(memory_space=pltpu.HBM)
    pieces = [
        (steps, block, features),
        (steps, block, positions, kv_features),
        (steps, block, positions, kv_features),
    ]
    return pl.pallas_call(
        functools.partial(attend_away_body, features // kv_features),
        in_specs=[hbm] * 4,
        out_specs=[vmem_spec] * 5,
        out_shape=[
            jax.ShapeDtypeStruct((rows, features), jnp.float32),
            jax.ShapeDtypeStruct((rows, LANES), jnp.float32),
        ]
        + [jax.ShapeDtypeStruct(shape, jnp.bfloat16) for shape in pieces],
        scratch_shapes=[pltpu.VMEM(shape, jnp.bfloat16) for shape in pieces]
        + [
            pltpu.SMEM((rows,), jnp.int32),
            pltpu.SemaphoreType.DMA((6, steps)),
            pltpu.SemaphoreType.DMA,
        ],
        compiler_params=pltpu.CompilerParams(vmem_limit_bytes=16 * MIB),
        cost_estimate=light,
        name="attend_away",
    )(
        *(
            pltpu.with_memory_space_constraint(a, pltpu.HBM)
            for a in (lengths, queries, keys, values)
        )
    )


def attend_own(queries, keys, values, lengths):
    steps, block, features = queries.shape
    group = features // keys.shape[3]
    return pl.pallas_call(
        functools.partial(attend_own_body, group),
        in_specs=[pl.BlockSpec(memory_space=pltpu.SMEM)] + [vmem_spec] * 3,
        out_specs=[vmem_spec] * 2,
        out_shape=[
            jax.ShapeDtypeStruct((steps * block, features), jnp.float32),
            jax.ShapeDtypeStruct((steps * block, LANES), jnp.float32),
        ],
        compiler_params=pltpu.CompilerParams(vmem_limit_bytes=12 * MIB),
        cost_estimate=light,
        name="attend_own",
    )(lengths, queries, keys, values)


def places(ids, target, owned_count):
    rows = ids.shape[0]
    member = ids - target * owned_count
    owned = (member >= 0) & (member < owned_count)
    mark = jnp.where(owned, 1.0, 0.0)
    earlier = lax.broadcasted_iota(jnp.int32, (rows, rows), 1) < lax.broadcasted_iota(
        jnp.int32, (rows, rows), 0
    )
    before = jnp.dot(
        jnp.where(earlier, 1.0, 0.0).astype(jnp.bfloat16),
        mark.astype(jnp.bfloat16),
        preferred_element_type=jnp.float32,
    )
    count = jnp.sum(mark, axis=0, keepdims=True)
    row = lax.broadcasted_iota(jnp.int32, ids.shape, 0).astype(jnp.float32)
    return jnp.where(owned, before, count + row - before)


def merge_body(shifts, owned_count, own_ref, own_level, other_ref, other_level, ids_ref, out_ref, *fronts):
    rows = own_ref.shape[0]
    share = 1.0 / (1.0 + jnp.exp2(own_level[...] - other_level[...]))
    for j in range(own_ref.shape[1] // HD):
        at = slice(j * HD, (j + 1) * HD)
        own = own_ref[:, at]
        other = other_ref[:, at].astype(jnp.float32)
        out_ref[:, at] = (own + (other - own) * share[:, j : j + 1]).astype(out_ref.dtype)
    for shift, ref in zip(shifts, fronts):
        route_to(shift, owned_count, ids_ref, out_ref, ref, 0)


def route_to(shift, owned_count, ids_ref, rows_ref, out_ref, first):
    rows, slots = rows_ref.shape[0], out_ref.shape[0]
    me = lax.axis_index("adapter")
    ids = ids_ref[pl.ds(pl.multiple_of(me * rows, 16), rows), :]
    place = places(ids, lax.bitwise_xor(me, shift), owned_count).T
    slot = lax.broadcasted_iota(jnp.int32, (slots, rows), 0) + first
    take = jnp.where(place[:slots, :] == slot.astype(jnp.float32), 1.0, 0.0)
    out_ref[...] = jnp.dot(
        take.astype(jnp.bfloat16), rows_ref[...], preferred_element_type=jnp.float32
    ).astype(out_ref.dtype)


def merge(own, own_level, other, other_level, ids, owned_count, shifts, capacity):
    shapes = [own.shape] + [(capacity, own.shape[1])] * len(shifts)
    return pl.pallas_call(
        functools.partial(merge_body, shifts, owned_count),
        in_specs=[vmem_spec] * 5,
        out_specs=[vmem_spec] * len(shapes),
        out_shape=[jax.ShapeDtypeStruct(s, jnp.bfloat16) for s in shapes],
        compiler_params=pltpu.CompilerParams(vmem_limit_bytes=10 * MIB),
        cost_estimate=light,
        name="merge",
    )(own, own_level, other, other_level, ids)


def route_rest_body(first, shifts, owned_count, ids_ref, rows_ref, _, *outs):
    for shift, ref in zip(shifts, outs):
        route_to(shift, owned_count, ids_ref, rows_ref, ref, first)


def route_rest(ids, rows, after, first, owned_count, shifts):
    shape = (rows.shape[0] - first, rows.shape[1])
    return pl.pallas_call(
        functools.partial(route_rest_body, first, shifts, owned_count),
        in_specs=[vmem_spec] * 2 + [pl.BlockSpec(memory_space=pl.ANY)],
        out_specs=[vmem_spec] * len(shifts),
        out_shape=[jax.ShapeDtypeStruct(shape, jnp.bfloat16)] * len(shifts),
        compiler_params=pltpu.CompilerParams(vmem_limit_bytes=6 * MIB),
        cost_estimate=light,
        name="route_rest",
    )(ids, rows, after)


def put_back(ids, source, part, first, owned_count):
    rows, slots = ids.shape[0], part.shape[0]
    me = lax.axis_index("adapter")
    place = places(ids, me, owned_count)
    slot = lax.broadcasted_iota(jnp.int32, (rows, slots), 1) + first
    put = jnp.where(place[:, :slots] == slot.astype(jnp.float32), 1.0, 0.0)
    return jnp.dot(put.astype(jnp.bfloat16), part, preferred_element_type=jnp.float32)


def join_body(count, *refs):
    for j, ref in enumerate(refs[:count]):
        refs[-1][j] = ref[...]


def join(parts, after=()):
    shape = (len(parts), *parts[0].shape)
    return pl.pallas_call(
        functools.partial(join_body, len(parts)),
        in_specs=[vmem_spec] * len(parts) + [pl.BlockSpec(memory_space=pl.ANY)] * len(after),
        out_specs=vmem_spec,
        out_shape=jax.ShapeDtypeStruct(shape, parts[0].dtype),
        compiler_params=pltpu.CompilerParams(vmem_limit_bytes=4 * MIB),
        cost_estimate=pl.CostEstimate(flops=1000, bytes_accessed=1000, transcendentals=0),
        name="join",
    )(*parts, *after)


def restore_body(shifts, owned_count, ids_ref, *refs):
    count, outs = len(shifts), refs[-2:]
    rows = outs[0].shape[0] // count
    slots = refs[0].shape[1]
    for j, shift in enumerate(shifts):
        source = lax.bitwise_xor(lax.axis_index("adapter"), shift)
        ids = ids_ref[pl.ds(pl.multiple_of(source * rows, 16), rows), :]
        for n, out_ref in enumerate(outs):
            front = put_back(ids, source, refs[2 * n][j], 0, owned_count)
            back = put_back(ids, source, refs[2 * n + 1][j], slots, owned_count)
            out_ref[j * rows : (j + 1) * rows, :] = (front + back).astype(out_ref.dtype)


def restore(ids, own, other, after, owned_count, shifts):
    count = len(shifts)
    rows, features = own[0].shape[1] + own[1].shape[1], own[0].shape[2]
    return pl.pallas_call(
        functools.partial(restore_body, shifts, owned_count),
        in_specs=[vmem_spec] * 5 + [pl.BlockSpec(memory_space=pl.ANY)],
        out_specs=[vmem_spec] * 2,
        out_shape=[jax.ShapeDtypeStruct((count * rows, features), jnp.bfloat16)] * 2,
        compiler_params=pltpu.CompilerParams(vmem_limit_bytes=8 * MIB),
        cost_estimate=light,
        name="restore",
    )(ids, *own, *other, after)


def down_body(count, plain, rank, owned_count, ids_ref, own_ref, *refs):
    xs, (out_ref, picked_ref) = refs[:count], refs[-2:]
    me = lax.axis_index("adapter")
    rows = out_ref.shape[0] * 2 // count
    width = own_ref.shape[0]
    transposed = (((1,), (1,)), ((), ()))
    x = jnp.concatenate([r[...] for r in xs], axis=0) if count > 1 else xs[0][...]
    product = lax.dot_general(x, own_ref[...], transposed, preferred_element_type=jnp.float32)
    per_tile = LANES // rank
    first = 0
    for j in range(count):
        source = lax.bitwise_xor(me, j) if count > 1 else 0
        at = pl.ds(pl.multiple_of(source * rows, 16), rows)
        ids = ids_ref[at, :]
        member = ids - me * owned_count
        slots = xs[j].shape[0]
        if j >= plain:
            place = places(ids, me, owned_count)
            slot = lax.broadcasted_iota(jnp.int32, (slots, rows), 0).astype(jnp.float32)
            take = jnp.where(place.T[:slots, :] == slot, 1.0, 0.0).astype(jnp.bfloat16)
            member = jnp.dot(
                take,
                member.astype(jnp.float32).astype(jnp.bfloat16),
                preferred_element_type=jnp.float32,
            ).astype(jnp.int32)
        lane = lax.broadcasted_iota(jnp.int32, (slots, LANES), 1)
        picked = jnp.zeros((slots, LANES), jnp.float32)
        for t in range(width // LANES):
            part = product[first : first + slots, t * LANES : (t + 1) * LANES]
            picked += jnp.where(member == t * per_tile + lane // rank, part, 0.0)
        first += slots
        if j >= plain:
            slot = lax.broadcasted_iota(jnp.int32, (rows, slots), 1).astype(jnp.float32)
            put = jnp.where(place[:, :slots] == slot, 1.0, 0.0)
            picked = jnp.dot(
                put, picked, precision=lax.Precision.HIGHEST, preferred_element_type=jnp.float32
            )
        picked_ref[at, :] = picked + pltpu.roll(picked, rank, 1)
    packed = out_ref.shape[0]
    left = lax.broadcasted_iota(jnp.int32, (packed, LANES), 1) < rank
    out_ref[...] = jnp.where(left, picked_ref[:packed, :], picked_ref[packed:, :])


def down(ids, weight, owned_count, rank, own, plain, after=()):
    count, rows = len(own), ids.shape[0]
    return pl.pallas_call(
        functools.partial(down_body, count, plain, rank, owned_count),
        in_specs=[vmem_spec] * (2 + count) + [pl.BlockSpec(memory_space=pl.ANY)] * len(after),
        out_specs=vmem_spec,
        out_shape=jax.ShapeDtypeStruct((rows // 2, LANES), jnp.float32),
        scratch_shapes=[pltpu.VMEM((rows, LANES), jnp.float32)],
        compiler_params=pltpu.CompilerParams(vmem_limit_bytes=16 * MIB),
        cost_estimate=light,
        name="down",
    )(ids, weight, *own, *after)


def up_body(count, rank, which, with_residual, ids_ref, base_ref, up_ref, *refs):
    mids, out_ref = refs[:count], refs[-1]
    side = lax.axis_index("mp")
    packed = mids[0][...].astype(jnp.float32)
    for r in mids[1:]:
        packed += r[...].astype(jnp.float32)
    packed = packed.astype(jnp.bfloat16).astype(jnp.float32)
    turned = pltpu.roll(packed, rank, 1)
    rows = out_ref.shape[0]
    left = lax.broadcasted_iota(jnp.int32, packed.shape, 1) < rank
    if which == "all":
        at = pl.ds(0, rows)
        total = jnp.concatenate(
            [jnp.where(left, packed, turned), jnp.where(left, turned, packed)], axis=0
        )
    else:
        part = side if which == "mine" else 1 - side
        at = pl.ds(pl.multiple_of(part * rows, 16), rows)
        total = jnp.where(left == (part == 0), packed, turned)
    lane = lax.broadcasted_iota(jnp.int32, (rows, LANES), 1)
    per_tile = LANES // rank
    local = ids_ref[at, :] - side * (up_ref.shape[0] // rank)
    spread = jnp.concatenate(
        [
            jnp.where(local == t * per_tile + lane // rank, total, 0.0)
            for t in range(up_ref.shape[0] // LANES)
        ],
        axis=1,
    ).astype(jnp.bfloat16)
    delta = jnp.dot(spread, up_ref[...], preferred_element_type=jnp.float32)
    out = base_ref[at, :] + adapter_scale * delta
    if with_residual:
        out += refs[count][...].astype(jnp.float32)
    out_ref[...] = out.astype(out_ref.dtype)


def up(ids, base, weight, mids, which, rows, residual, out_type):
    rank = weight.shape[1]
    flat = weight.reshape(-1, weight.shape[2])
    extra = [] if residual is None else [residual]
    return pl.pallas_call(
        functools.partial(up_body, len(mids), rank, which, residual is not None),
        in_specs=[vmem_spec] * (3 + len(mids) + len(extra)),
        out_specs=vmem_spec,
        out_shape=jax.ShapeDtypeStruct((rows, base.shape[1]), out_type),
        compiler_params=pltpu.CompilerParams(
            vmem_limit_bytes=(24 if which == "all" else 10) * MIB
        ),
        cost_estimate=light,
        name="up",
    )(ids, base, flat, *mids, *extra)


def last_body(kept_ref, back_ref, out_ref):
    out_ref[...] = (kept_ref[...] + back_ref[...].astype(jnp.float32)).astype(out_ref.dtype)


def last(kept, back):
    return pl.pallas_call(
        last_body,
        in_specs=[vmem_spec] * 2,
        out_specs=vmem_spec,
        out_shape=jax.ShapeDtypeStruct(kept.shape, jnp.bfloat16),
        compiler_params=pltpu.CompilerParams(vmem_limit_bytes=4 * MIB),
        name="last",
    )(kept, back)


def base_body(count, unit, tile, w_ref, *refs):
    xs, ys, out_ref = refs[:count], refs[count : 2 * count], refs[-1]
    me, half = lax.axis_index("adapter"), lax.axis_index("kv")
    depth = xs[0].shape[1]
    x = jnp.concatenate([r[...] for r in xs], axis=0) if count > 1 else xs[0][...]
    y = jnp.concatenate([r[...] for r in ys], axis=0) if count > 1 else ys[0][...]
    own = pl.ds(pl.multiple_of(half * depth, depth), depth)
    other = pl.ds(pl.multiple_of((1 - half) * depth, depth), depth)
    for t in range(out_ref.shape[1] // tile):
        at = slice(t * tile, (t + 1) * tile)
        out = jnp.dot(x, w_ref[own, at], preferred_element_type=jnp.float32)
        out += jnp.dot(y, w_ref[other, at], preferred_element_type=jnp.float32)
        for j in range(out.shape[0] // unit):
            source = lax.bitwise_xor(me, j) if count > 1 else 0
            block = pl.ds(pl.multiple_of(source * unit, 16), unit)
            out_ref[block, at] = out[j * unit : (j + 1) * unit]


def base_projection(weight, own, other):
    count = len(own)
    rows = sum(b.shape[0] for b in own)
    columns = weight.shape[1]
    unit = own[0].shape[0]
    return pl.pallas_call(
        functools.partial(base_body, count, unit, min(256, columns)),
        in_specs=[vmem_spec] * (1 + 2 * count),
        out_specs=vmem_spec,
        out_shape=jax.ShapeDtypeStruct((rows, columns), jnp.float32),
        compiler_params=pltpu.CompilerParams(vmem_limit_bytes=24 * MIB),
        cost_estimate=light,
        name="base",
    )(weight, *own, *other)


def swapped(x, axis, other=1):
    return lax.ppermute(x, axis, [(i, i ^ other) for i in range(lax.axis_size(axis))])


def local(
    queries,
    keys,
    values,
    lengths,
    row_adapter_index,
    residual,
    output_weight,
    adapter_down_weight,
    adapter_up_weight,
):
    owners, splits = lax.axis_size("adapter"), lax.axis_size("mp")
    entire_rows = row_adapter_index.shape[0]
    kept_rows = entire_rows // splits
    direct = owners == 4 and splits == 2
    owned_count = adapter_down_weight.shape[0]
    capacity = 2 * queries.shape[0] // owners
    ids = jnp.broadcast_to(row_adapter_index[:, None], (entire_rows, LANES))

    sent, sent_level, *own_operands = attend_away(queries, keys, values, lengths)
    got, got_level = swapped(sent, "kv"), swapped(sent_level, "kv")
    own, own_level = attend_own(*own_operands, lengths)
    shifts = tuple(range(2, owners)) if direct else ()
    attended, *fronts = merge(
        own, own_level, got, got_level, ids, owned_count, shifts, capacity
    )

    rank = adapter_down_weight.shape[2]
    down_own = jnp.transpose(adapter_down_weight, (0, 2, 1)).reshape(-1, attended.shape[1])
    if direct:
        fronts = [swapped(f, "adapter", j) for j, f in zip(shifts, fronts)]
        beside = swapped(attended, "adapter", 1)
        own = [attended, beside]
        other = [swapped(b, "kv") for b in own]
        backs = route_rest(ids, attended, fronts[0], capacity, owned_count, shifts)
        part = down(ids, down_own, owned_count, rank, own + fronts, 2, backs[:1])
        backs = [swapped(b, "adapter", j) for j, b in zip(shifts, backs)]
        routed = [join(fronts), join(backs, ())]
        part = part + swapped(part, "mp")
        part = (part + swapped(part, "kv")).astype(jnp.bfloat16)
        mids = [part] + [swapped(part, "adapter", j) for j in range(1, owners)]
        own_rest, other_rest = restore(
            ids, routed, [swapped(r, "kv") for r in routed], part, owned_count, shifts
        )
        base = base_projection(output_weight, own + [own_rest], other + [other_rest])
        away = up(
            ids, base, adapter_up_weight, mids, "theirs", kept_rows, None, jnp.bfloat16
        )
        back = swapped(away, "mp")
        kept = up(
            ids, base, adapter_up_weight, mids, "mine", kept_rows, residual, jnp.float32
        )
        return last(kept, back)
    blocks = lax.all_gather(attended, "adapter", axis=0, tiled=True)
    others = swapped(blocks, "kv")
    part = down(ids, down_own, owned_count, rank, [blocks], 1)
    mids = [lax.psum(part, ("adapter", "mp", "kv"))]
    base = base_projection(output_weight, [blocks], [others])
    terms = up(ids, base, adapter_up_weight, mids, "all", entire_rows, None, jnp.float32)
    summed = lax.psum_scatter(terms, "mp", scatter_dimension=0, tiled=True)
    return (residual.astype(jnp.float32) + summed).astype(jnp.bfloat16)


def solution(mesh):
    placed = (
        P(("groups", "adapter"), "mp"),
        P(("groups", "adapter"), "kv", "mp"),
        P(("groups", "adapter"), "kv", "mp"),
        P(("groups", "adapter")),
        P("groups"),
        P(("groups", "mp"), ("adapter", "kv")),
        P("mp", ("adapter", "kv")),
        P("adapter", ("mp", "kv"), None),
        P("mp", None, ("adapter", "kv")),
    )
    return jax.shard_map(
        local,
        mesh=mesh,
        in_specs=placed,
        out_specs=P(("groups", "mp"), ("adapter", "kv")),
        check_vma=False,
    )
```

```python
import functools
import math

import jax
import jax.numpy as jnp
from jax import lax
from jax.experimental import pallas as pl
from jax.experimental.pallas import tpu as pltpu
from jax.sharding import PartitionSpec as P

HD = 128
LANES = 128
MIB = 1 << 20

neg_big = -1e30
adapter_scale = 2.0
score_scale = 1.0 / math.sqrt(HD)
log2_e = 1.4426950408889634


vmem_spec = pl.BlockSpec(memory_space=pltpu.VMEM)
light = pl.CostEstimate(flops=1000, bytes_accessed=1000, transcendentals=0)


def attend_away_body(group, lengths_hbm, q_hbm, k_hbm, v_hbm, o_ref, s_ref, *refs):
    own, fetched, (lengths, sems, sem) = refs[:3], refs[3:6], refs[6:]
    core = lax.axis_index("kv")
    steps, rows = own[0].shape[:2]

    def copies(half, dst, first, i):
        at = pl.ds(i * rows, rows)
        for n, (hbm, ref) in enumerate(zip((q_hbm, k_hbm, v_hbm), dst)):
            width = ref.shape[-1]
            columns = pl.ds(pl.multiple_of(half * width, width), width)
            src = hbm.at[at, columns] if n == 0 else hbm.at[at, :, columns]
            yield pltpu.make_async_copy(src, ref.at[i], sems.at[first + n, i])

    number = pltpu.make_async_copy(lengths_hbm, lengths, sem)
    number.start()
    for half, dst, first in ((1 - core, fetched, 0), (core, own, 3)):
        for i in range(steps):
            for copy in copies(half, dst, first, i):
                copy.start()
    number.wait()
    for i in range(steps):
        for copy in copies(1 - core, fetched, 0, i):
            copy.wait()
        attend_block(group, core, i, lengths, *fetched, o_ref, s_ref)
    for i in range(steps):
        for copy in copies(core, own, 3, i):
            copy.wait()


def attend_own_body(group, lengths, q_ref, k_ref, v_ref, o_ref, s_ref):
    for i in range(q_ref.shape[0]):
        attend_block(group, lax.axis_index("kv"), i, lengths, q_ref, k_ref, v_ref, o_ref, s_ref)


def attend_block(group, core, i, lengths, q_ref, k_ref, v_ref, o_ref, s_ref):
    positions = k_ref.shape[2]
    rows, kv_heads = q_ref.shape[1], k_ref.shape[3] // HD
    offset = core * positions
    wide = 8 * positions
    row_id = lax.broadcasted_iota(jnp.int32, (8, wide), 0)
    column = lax.broadcasted_iota(jnp.int32, (8, wide), 1)
    own_row = column // positions == row_id
    position = column % positions + offset
    lane = lax.broadcasted_iota(jnp.int32, (8, LANES), 1)
    ones = jnp.ones((wide, LANES), jnp.bfloat16)
    queries = q_ref[i].astype(jnp.float32)
    outs = {}
    stats = []
    for sub in range(rows // 8):
        limit = jnp.zeros((8, wide), jnp.int32)
        for t in range(8):
            limit = jnp.where(row_id == t, lengths[i * rows + sub * 8 + t], limit)
        valid = own_row & (position < limit)
        stat = jnp.zeros((8, LANES), jnp.float32)
        for g in range(kv_heads):
            q = jnp.concatenate(
                [
                    queries[sub * 8 : sub * 8 + 8, j * HD : (j + 1) * HD]
                    for j in range(g * group, (g + 1) * group)
                ],
                axis=0,
            ).astype(jnp.bfloat16)
            k = k_ref[i, sub * 8 : sub * 8 + 8, :, g * HD : (g + 1) * HD].reshape(wide, HD)
            v = v_ref[i, sub * 8 : sub * 8 + 8, :, g * HD : (g + 1) * HD].reshape(wide, HD)
            scores = lax.dot_general(
                q, k, (((1,), (1,)), ((), ())), preferred_element_type=jnp.float32
            ).reshape(group, 8, wide)
            scores = jnp.where(valid[None], scores, neg_big)
            top = jnp.max(scores, axis=2, keepdims=True)
            weights = jnp.exp2((scores - top) * (score_scale * log2_e))
            weights = weights.astype(jnp.bfloat16).reshape(group * 8, wide)
            both = jnp.dot(
                weights,
                jnp.concatenate([v, ones], axis=1),
                preferred_element_type=jnp.float32,
            )
            total = both[:, HD:]
            out = both[:, :HD] / total
            level = jnp.log2(total) + top.reshape(group * 8, 1) * (score_scale * log2_e)
            for j in range(group):
                outs[sub, g * group + j] = out[j * 8 : j * 8 + 8]
                stat = jnp.where(lane == g * group + j, level[j * 8 : j * 8 + 8], stat)
        stats.append(stat)
    at = slice(i * rows, (i + 1) * rows)
    for j in range(kv_heads * group):
        o_ref[at, j * HD : (j + 1) * HD] = jnp.concatenate(
            [outs[sub, j] for sub in range(rows // 8)], axis=0
        ).astype(o_ref.dtype)
    s_ref[at, :] = jnp.concatenate(stats, axis=0)


def attend_away(queries, keys, values, lengths):
    rows, features = queries.shape[0], queries.shape[1] // 2
    positions, kv_features = keys.shape[1], keys.shape[2] // 2
    block = 16
    steps = rows // block
    hbm = pl.BlockSpec(memory_space=pltpu.HBM)
    pieces = [
        (steps, block, features),
        (steps, block, positions, kv_features),
        (steps, block, positions, kv_features),
    ]
    return pl.pallas_call(
        functools.partial(attend_away_body, features // kv_features),
        in_specs=[hbm] * 4,
        out_specs=[vmem_spec] * 5,
        out_shape=[
            jax.ShapeDtypeStruct((rows, features), jnp.float32),
            jax.ShapeDtypeStruct((rows, LANES), jnp.float32),
        ]
        + [jax.ShapeDtypeStruct(shape, jnp.bfloat16) for shape in pieces],
        scratch_shapes=[pltpu.VMEM(shape, jnp.bfloat16) for shape in pieces]
        + [
            pltpu.SMEM((rows,), jnp.int32),
            pltpu.SemaphoreType.DMA((6, steps)),
            pltpu.SemaphoreType.DMA,
        ],
        compiler_params=pltpu.CompilerParams(vmem_limit_bytes=16 * MIB),
        cost_estimate=light,
        name="attend_away",
    )(
        *(
            pltpu.with_memory_space_constraint(a, pltpu.HBM)
            for a in (lengths, queries, keys, values)
        )
    )


def attend_own(queries, keys, values, lengths):
    steps, block, features = queries.shape
    group = features // keys.shape[3]
    return pl.pallas_call(
        functools.partial(attend_own_body, group),
        in_specs=[pl.BlockSpec(memory_space=pltpu.SMEM)] + [vmem_spec] * 3,
        out_specs=[vmem_spec] * 2,
        out_shape=[
            jax.ShapeDtypeStruct((steps * block, features), jnp.float32),
            jax.ShapeDtypeStruct((steps * block, LANES), jnp.float32),
        ],
        compiler_params=pltpu.CompilerParams(vmem_limit_bytes=12 * MIB),
        cost_estimate=light,
        name="attend_own",
    )(lengths, queries, keys, values)


def places(ids, target, owned_count):
    rows = ids.shape[0]
    member = ids - target * owned_count
    owned = (member >= 0) & (member < owned_count)
    mark = jnp.where(owned, 1.0, 0.0)
    earlier = lax.broadcasted_iota(jnp.int32, (rows, rows), 1) < lax.broadcasted_iota(
        jnp.int32, (rows, rows), 0
    )
    before = jnp.dot(
        jnp.where(earlier, 1.0, 0.0).astype(jnp.bfloat16),
        mark.astype(jnp.bfloat16),
        preferred_element_type=jnp.float32,
    )
    count = jnp.sum(mark, axis=0, keepdims=True)
    row = lax.broadcasted_iota(jnp.int32, ids.shape, 0).astype(jnp.float32)
    return jnp.where(owned, before, count + row - before)


def merge_body(shifts, owned_count, own_ref, own_level, other_ref, other_level, ids_ref, out_ref, *fronts):
    rows = own_ref.shape[0]
    share = 1.0 / (1.0 + jnp.exp2(own_level[...] - other_level[...]))
    for j in range(own_ref.shape[1] // HD):
        at = slice(j * HD, (j + 1) * HD)
        own = own_ref[:, at]
        other = other_ref[:, at].astype(jnp.float32)
        out_ref[:, at] = (own + (other - own) * share[:, j : j + 1]).astype(out_ref.dtype)
    for shift, ref in zip(shifts, fronts):
        route_to(shift, owned_count, ids_ref, out_ref, ref, 0)


def route_to(shift, owned_count, ids_ref, rows_ref, out_ref, first):
    rows, slots = rows_ref.shape[0], out_ref.shape[0]
    me = lax.axis_index("adapter")
    ids = ids_ref[pl.ds(pl.multiple_of(me * rows, 16), rows), :]
    place = places(ids, lax.bitwise_xor(me, shift), owned_count).T
    slot = lax.broadcasted_iota(jnp.int32, (slots, rows), 0) + first
    take = jnp.where(place[:slots, :] == slot.astype(jnp.float32), 1.0, 0.0)
    out_ref[...] = jnp.dot(
        take.astype(jnp.bfloat16), rows_ref[...], preferred_element_type=jnp.float32
    ).astype(out_ref.dtype)


def merge(own, own_level, other, other_level, ids, owned_count, shifts, capacity):
    shapes = [own.shape] + [(capacity, own.shape[1])] * len(shifts)
    return pl.pallas_call(
        functools.partial(merge_body, shifts, owned_count),
        in_specs=[vmem_spec] * 5,
        out_specs=[vmem_spec] * len(shapes),
        out_shape=[jax.ShapeDtypeStruct(s, jnp.bfloat16) for s in shapes],
        compiler_params=pltpu.CompilerParams(vmem_limit_bytes=10 * MIB),
        cost_estimate=light,
        name="merge",
    )(own, own_level, other, other_level, ids)


def route_rest_body(first, shifts, owned_count, ids_ref, rows_ref, _, *outs):
    for shift, ref in zip(shifts, outs):
        route_to(shift, owned_count, ids_ref, rows_ref, ref, first)


def route_rest(ids, rows, after, first, owned_count, shifts):
    shape = (rows.shape[0] - first, rows.shape[1])
    return pl.pallas_call(
        functools.partial(route_rest_body, first, shifts, owned_count),
        in_specs=[vmem_spec] * 2 + [pl.BlockSpec(memory_space=pl.ANY)],
        out_specs=[vmem_spec] * len(shifts),
        out_shape=[jax.ShapeDtypeStruct(shape, jnp.bfloat16)] * len(shifts),
        compiler_params=pltpu.CompilerParams(vmem_limit_bytes=6 * MIB),
        cost_estimate=light,
        name="route_rest",
    )(ids, rows, after)


def put_back(ids, source, part, first, owned_count):
    rows, slots = ids.shape[0], part.shape[0]
    me = lax.axis_index("adapter")
    place = places(ids, me, owned_count)
    slot = lax.broadcasted_iota(jnp.int32, (rows, slots), 1) + first
    put = jnp.where(place[:, :slots] == slot.astype(jnp.float32), 1.0, 0.0)
    return jnp.dot(put.astype(jnp.bfloat16), part, preferred_element_type=jnp.float32)


def join_body(count, *refs):
    for j, ref in enumerate(refs[:count]):
        refs[-1][j] = ref[...]


def join(parts, after=()):
    shape = (len(parts), *parts[0].shape)
    return pl.pallas_call(
        functools.partial(join_body, len(parts)),
        in_specs=[vmem_spec] * len(parts) + [pl.BlockSpec(memory_space=pl.ANY)] * len(after),
        out_specs=vmem_spec,
        out_shape=jax.ShapeDtypeStruct(shape, parts[0].dtype),
        compiler_params=pltpu.CompilerParams(vmem_limit_bytes=4 * MIB),
        cost_estimate=pl.CostEstimate(flops=1000, bytes_accessed=1000, transcendentals=0),
        name="join",
    )(*parts, *after)


def restore_body(shifts, owned_count, ids_ref, *refs):
    count, outs = len(shifts), refs[-2:]
    rows = outs[0].shape[0] // count
    slots = refs[0].shape[1]
    for j, shift in enumerate(shifts):
        source = lax.bitwise_xor(lax.axis_index("adapter"), shift)
        ids = ids_ref[pl.ds(pl.multiple_of(source * rows, 16), rows), :]
        for n, out_ref in enumerate(outs):
            front = put_back(ids, source, refs[2 * n][j], 0, owned_count)
            back = put_back(ids, source, refs[2 * n + 1][j], slots, owned_count)
            out_ref[j * rows : (j + 1) * rows, :] = (front + back).astype(out_ref.dtype)


def restore(ids, own, other, after, owned_count, shifts):
    count = len(shifts)
    rows, features = own[0].shape[1] + own[1].shape[1], own[0].shape[2]
    return pl.pallas_call(
        functools.partial(restore_body, shifts, owned_count),
        in_specs=[vmem_spec] * 5 + [pl.BlockSpec(memory_space=pl.ANY)],
        out_specs=[vmem_spec] * 2,
        out_shape=[jax.ShapeDtypeStruct((count * rows, features), jnp.bfloat16)] * 2,
        compiler_params=pltpu.CompilerParams(vmem_limit_bytes=8 * MIB),
        cost_estimate=light,
        name="restore",
    )(ids, *own, *other, after)


def down_body(count, plain, rank, owned_count, ids_ref, own_ref, *refs):
    xs, (out_ref, picked_ref) = refs[:count], refs[-2:]
    me = lax.axis_index("adapter")
    rows = out_ref.shape[0] * 2 // count
    width = own_ref.shape[0]
    transposed = (((1,), (1,)), ((), ()))
    x = jnp.concatenate([r[...] for r in xs], axis=0) if count > 1 else xs[0][...]
    product = lax.dot_general(x, own_ref[...], transposed, preferred_element_type=jnp.float32)
    per_tile = LANES // rank
    first = 0
    for j in range(count):
        source = lax.bitwise_xor(me, j) if count > 1 else 0
        at = pl.ds(pl.multiple_of(source * rows, 16), rows)
        ids = ids_ref[at, :]
        member = ids - me * owned_count
        slots = xs[j].shape[0]
        if j >= plain:
            place = places(ids, me, owned_count)
            slot = lax.broadcasted_iota(jnp.int32, (slots, rows), 0).astype(jnp.float32)
            take = jnp.where(place.T[:slots, :] == slot, 1.0, 0.0).astype(jnp.bfloat16)
            member = jnp.dot(
                take,
                member.astype(jnp.float32).astype(jnp.bfloat16),
                preferred_element_type=jnp.float32,
            ).astype(jnp.int32)
        lane = lax.broadcasted_iota(jnp.int32, (slots, LANES), 1)
        picked = jnp.zeros((slots, LANES), jnp.float32)
        for t in range(width // LANES):
            part = product[first : first + slots, t * LANES : (t + 1) * LANES]
            picked += jnp.where(member == t * per_tile + lane // rank, part, 0.0)
        first += slots
        if j >= plain:
            slot = lax.broadcasted_iota(jnp.int32, (rows, slots), 1).astype(jnp.float32)
            put = jnp.where(place[:, :slots] == slot, 1.0, 0.0)
            picked = jnp.dot(
                put, picked, precision=lax.Precision.HIGHEST, preferred_element_type=jnp.float32
            )
        picked_ref[at, :] = picked + pltpu.roll(picked, rank, 1)
    packed = out_ref.shape[0]
    left = lax.broadcasted_iota(jnp.int32, (packed, LANES), 1) < rank
    out_ref[...] = jnp.where(left, picked_ref[:packed, :], picked_ref[packed:, :])


def down(ids, weight, owned_count, rank, own, plain, after=()):
    count, rows = len(own), ids.shape[0]
    return pl.pallas_call(
        functools.partial(down_body, count, plain, rank, owned_count),
        in_specs=[vmem_spec] * (2 + count) + [pl.BlockSpec(memory_space=pl.ANY)] * len(after),
        out_specs=vmem_spec,
        out_shape=jax.ShapeDtypeStruct((rows // 2, LANES), jnp.float32),
        scratch_shapes=[pltpu.VMEM((rows, LANES), jnp.float32)],
        compiler_params=pltpu.CompilerParams(vmem_limit_bytes=16 * MIB),
        cost_estimate=light,
        name="down",
    )(ids, weight, *own, *after)


def up_body(count, rank, which, with_residual, ids_ref, base_ref, up_ref, *refs):
    mids, out_ref = refs[:count], refs[-1]
    side = lax.axis_index("mp")
    packed = mids[0][...].astype(jnp.float32)
    for r in mids[1:]:
        packed += r[...].astype(jnp.float32)
    packed = packed.astype(jnp.bfloat16).astype(jnp.float32)
    turned = pltpu.roll(packed, rank, 1)
    rows = out_ref.shape[0]
    left = lax.broadcasted_iota(jnp.int32, packed.shape, 1) < rank
    if which == "all":
        at = pl.ds(0, rows)
        total = jnp.concatenate(
            [jnp.where(left, packed, turned), jnp.where(left, turned, packed)], axis=0
        )
    else:
        part = side if which == "mine" else 1 - side
        at = pl.ds(pl.multiple_of(part * rows, 16), rows)
        total = jnp.where(left == (part == 0), packed, turned)
    lane = lax.broadcasted_iota(jnp.int32, (rows, LANES), 1)
    per_tile = LANES // rank
    local = ids_ref[at, :] - side * (up_ref.shape[0] // rank)
    spread = jnp.concatenate(
        [
            jnp.where(local == t * per_tile + lane // rank, total, 0.0)
            for t in range(up_ref.shape[0] // LANES)
        ],
        axis=1,
    ).astype(jnp.bfloat16)
    delta = jnp.dot(spread, up_ref[...], preferred_element_type=jnp.float32)
    out = base_ref[at, :] + adapter_scale * delta
    if with_residual:
        out += refs[count][...].astype(jnp.float32)
    out_ref[...] = out.astype(out_ref.dtype)


def up(ids, base, weight, mids, which, rows, residual, out_type):
    rank = weight.shape[1]
    flat = weight.reshape(-1, weight.shape[2])
    extra = [] if residual is None else [residual]
    return pl.pallas_call(
        functools.partial(up_body, len(mids), rank, which, residual is not None),
        in_specs=[vmem_spec] * (3 + len(mids) + len(extra)),
        out_specs=vmem_spec,
        out_shape=jax.ShapeDtypeStruct((rows, base.shape[1]), out_type),
        compiler_params=pltpu.CompilerParams(
            vmem_limit_bytes=(24 if which == "all" else 10) * MIB
        ),
        cost_estimate=light,
        name="up",
    )(ids, base, flat, *mids, *extra)


def last_body(kept_ref, back_ref, out_ref):
    out_ref[...] = (kept_ref[...] + back_ref[...].astype(jnp.float32)).astype(out_ref.dtype)


def last(kept, back):
    return pl.pallas_call(
        last_body,
        in_specs=[vmem_spec] * 2,
        out_specs=vmem_spec,
        out_shape=jax.ShapeDtypeStruct(kept.shape, jnp.bfloat16),
        compiler_params=pltpu.CompilerParams(vmem_limit_bytes=4 * MIB),
        name="last",
    )(kept, back)


def base_body(count, unit, tile, w_ref, *refs):
    xs, ys, out_ref = refs[:count], refs[count : 2 * count], refs[-1]
    me, half = lax.axis_index("adapter"), lax.axis_index("kv")
    depth = xs[0].shape[1]
    x = jnp.concatenate([r[...] for r in xs], axis=0) if count > 1 else xs[0][...]
    y = jnp.concatenate([r[...] for r in ys], axis=0) if count > 1 else ys[0][...]
    own = pl.ds(pl.multiple_of(half * depth, depth), depth)
    other = pl.ds(pl.multiple_of((1 - half) * depth, depth), depth)
    for t in range(out_ref.shape[1] // tile):
        at = slice(t * tile, (t + 1) * tile)
        out = jnp.dot(x, w_ref[own, at], preferred_element_type=jnp.float32)
        out += jnp.dot(y, w_ref[other, at], preferred_element_type=jnp.float32)
        for j in range(out.shape[0] // unit):
            source = lax.bitwise_xor(me, j) if count > 1 else 0
            block = pl.ds(pl.multiple_of(source * unit, 16), unit)
            out_ref[block, at] = out[j * unit : (j + 1) * unit]


def base_projection(weight, own, other):
    count = len(own)
    rows = sum(b.shape[0] for b in own)
    columns = weight.shape[1]
    unit = own[0].shape[0]
    return pl.pallas_call(
        functools.partial(base_body, count, unit, min(256, columns)),
        in_specs=[vmem_spec] * (1 + 2 * count),
        out_specs=vmem_spec,
        out_shape=jax.ShapeDtypeStruct((rows, columns), jnp.float32),
        compiler_params=pltpu.CompilerParams(vmem_limit_bytes=24 * MIB),
        cost_estimate=light,
        name="base",
    )(weight, *own, *other)


def swapped(x, axis, other=1):
    return lax.ppermute(x, axis, [(i, i ^ other) for i in range(lax.axis_size(axis))])


def local(
    queries,
    keys,
    values,
    lengths,
    row_adapter_index,
    residual,
    output_weight,
    adapter_down_weight,
    adapter_up_weight,
):
    owners, splits = lax.axis_size("adapter"), lax.axis_size("mp")
    entire_rows = row_adapter_index.shape[0]
    kept_rows = entire_rows // splits
    direct = owners == 4 and splits == 2
    owned_count = adapter_down_weight.shape[0]
    capacity = 2 * queries.shape[0] // owners
    ids = jnp.broadcast_to(row_adapter_index[:, None], (entire_rows, LANES))

    sent, sent_level, *own_operands = attend_away(queries, keys, values, lengths)
    got, got_level = swapped(sent, "kv"), swapped(sent_level, "kv")
    own, own_level = attend_own(*own_operands, lengths)
    shifts = tuple(range(2, owners)) if direct else ()
    attended, *fronts = merge(
        own, own_level, got, got_level, ids, owned_count, shifts, capacity
    )

    rank = adapter_down_weight.shape[2]
    down_own = jnp.transpose(adapter_down_weight, (0, 2, 1)).reshape(-1, attended.shape[1])
    if direct:
        fronts = [swapped(f, "adapter", j) for j, f in zip(shifts, fronts)]
        beside = swapped(attended, "adapter", 1)
        own = [attended, beside]
        other = [swapped(b, "kv") for b in own]
        backs = route_rest(ids, attended, fronts[0], capacity, owned_count, shifts)
        part = down(ids, down_own, owned_count, rank, own + fronts, 2, [backs[0], other[0]])
        backs = [swapped(b, "adapter", j) for j, b in zip(shifts, backs)]
        routed = [join(fronts), join(backs, ())]
        part = part + swapped(part, "mp")
        part = (part + swapped(part, "kv")).astype(jnp.bfloat16)
        mids = [part] + [swapped(part, "adapter", j) for j in range(1, owners)]
        own_rest, other_rest = restore(
            ids, routed, [swapped(r, "kv") for r in routed], part, owned_count, shifts
        )
        base = base_projection(output_weight, own + [own_rest], other + [other_rest])
        away = up(
            ids, base, adapter_up_weight, mids, "theirs", kept_rows, None, jnp.bfloat16
        )
        back = swapped(away, "mp")
        kept = up(
            ids, base, adapter_up_weight, mids, "mine", kept_rows, residual, jnp.float32
        )
        return last(kept, back)
    blocks = lax.all_gather(attended, "adapter", axis=0, tiled=True)
    others = swapped(blocks, "kv")
    part = down(ids, down_own, owned_count, rank, [blocks], 1)
    mids = [lax.psum(part, ("adapter", "mp", "kv"))]
    base = base_projection(output_weight, [blocks], [others])
    terms = up(ids, base, adapter_up_weight, mids, "all", entire_rows, None, jnp.float32)
    summed = lax.psum_scatter(terms, "mp", scatter_dimension=0, tiled=True)
    return (residual.astype(jnp.float32) + summed).astype(jnp.bfloat16)


def solution(mesh):
    placed = (
        P(("groups", "adapter"), "mp"),
        P(("groups", "adapter"), "kv", "mp"),
        P(("groups", "adapter"), "kv", "mp"),
        P(("groups", "adapter")),
        P("groups"),
        P(("groups", "mp"), ("adapter", "kv")),
        P("mp", ("adapter", "kv")),
        P("adapter", ("mp", "kv"), None),
        P("mp", None, ("adapter", "kv")),
    )
    return jax.shard_map(
        local,
        mesh=mesh,
        in_specs=placed,
        out_specs=P(("groups", "mp"), ("adapter", "kv")),
        check_vma=False,
    )
```

```python
import functools
import math

import jax
import jax.numpy as jnp
from jax import lax
from jax.experimental import pallas as pl
from jax.experimental.pallas import tpu as pltpu
from jax.sharding import PartitionSpec as P

HD = 128
LANES = 128
MIB = 1 << 20

neg_big = -1e30
adapter_scale = 2.0
score_scale = 1.0 / math.sqrt(HD)
log2_e = 1.4426950408889634


vmem_spec = pl.BlockSpec(memory_space=pltpu.VMEM)
light = pl.CostEstimate(flops=1000, bytes_accessed=1000, transcendentals=0)


def attend_away_body(group, lengths_hbm, q_hbm, k_hbm, v_hbm, o_ref, s_ref, *refs):
    own, fetched, (lengths, sems, sem) = refs[:3], refs[3:6], refs[6:]
    core = lax.axis_index("kv")
    steps, rows = own[0].shape[:2]

    def copies(half, dst, first, i):
        at = pl.ds(i * rows, rows)
        for n, (hbm, ref) in enumerate(zip((q_hbm, k_hbm, v_hbm), dst)):
            width = ref.shape[-1]
            columns = pl.ds(pl.multiple_of(half * width, width), width)
            src = hbm.at[at, columns] if n == 0 else hbm.at[at, :, columns]
            yield pltpu.make_async_copy(src, ref.at[i], sems.at[first + n, i])

    number = pltpu.make_async_copy(lengths_hbm, lengths, sem)
    number.start()
    for half, dst, first in ((1 - core, fetched, 0), (core, own, 3)):
        for i in range(steps):
            for copy in copies(half, dst, first, i):
                copy.start()
    number.wait()
    for i in range(steps):
        for copy in copies(1 - core, fetched, 0, i):
            copy.wait()
        attend_block(group, core, i, lengths, *fetched, o_ref, s_ref)
    for i in range(steps):
        for copy in copies(core, own, 3, i):
            copy.wait()


def attend_own_body(group, lengths, q_ref, k_ref, v_ref, o_ref, s_ref):
    for i in range(q_ref.shape[0]):
        attend_block(group, lax.axis_index("kv"), i, lengths, q_ref, k_ref, v_ref, o_ref, s_ref)


def attend_block(group, core, i, lengths, q_ref, k_ref, v_ref, o_ref, s_ref):
    positions = k_ref.shape[2]
    rows, kv_heads = q_ref.shape[1], k_ref.shape[3] // HD
    offset = core * positions
    wide = 8 * positions
    row_id = lax.broadcasted_iota(jnp.int32, (8, wide), 0)
    column = lax.broadcasted_iota(jnp.int32, (8, wide), 1)
    own_row = column // positions == row_id
    position = column % positions + offset
    lane = lax.broadcasted_iota(jnp.int32, (8, LANES), 1)
    ones = jnp.ones((wide, LANES), jnp.bfloat16)
    queries = q_ref[i].astype(jnp.float32)
    outs = {}
    stats = []
    for sub in range(rows // 8):
        limit = jnp.zeros((8, wide), jnp.int32)
        for t in range(8):
            limit = jnp.where(row_id == t, lengths[i * rows + sub * 8 + t], limit)
        valid = own_row & (position < limit)
        stat = jnp.zeros((8, LANES), jnp.float32)
        for g in range(kv_heads):
            q = jnp.concatenate(
                [
                    queries[sub * 8 : sub * 8 + 8, j * HD : (j + 1) * HD]
                    for j in range(g * group, (g + 1) * group)
                ],
                axis=0,
            ).astype(jnp.bfloat16)
            k = k_ref[i, sub * 8 : sub * 8 + 8, :, g * HD : (g + 1) * HD].reshape(wide, HD)
            v = v_ref[i, sub * 8 : sub * 8 + 8, :, g * HD : (g + 1) * HD].reshape(wide, HD)
            scores = lax.dot_general(
                q, k, (((1,), (1,)), ((), ())), preferred_element_type=jnp.float32
            ).reshape(group, 8, wide)
            scores = jnp.where(valid[None], scores, neg_big)
            top = jnp.max(scores, axis=2, keepdims=True)
            weights = jnp.exp2((scores - top) * (score_scale * log2_e))
            weights = weights.astype(jnp.bfloat16).reshape(group * 8, wide)
            both = jnp.dot(
                weights,
                jnp.concatenate([v, ones], axis=1),
                preferred_element_type=jnp.float32,
            )
            total = both[:, HD:]
            out = both[:, :HD] / total
            level = jnp.log2(total) + top.reshape(group * 8, 1) * (score_scale * log2_e)
            for j in range(group):
                outs[sub, g * group + j] = out[j * 8 : j * 8 + 8]
                stat = jnp.where(lane == g * group + j, level[j * 8 : j * 8 + 8], stat)
        stats.append(stat)
    at = slice(i * rows, (i + 1) * rows)
    for j in range(kv_heads * group):
        o_ref[at, j * HD : (j + 1) * HD] = jnp.concatenate(
            [outs[sub, j] for sub in range(rows // 8)], axis=0
        ).astype(o_ref.dtype)
    s_ref[at, :] = jnp.concatenate(stats, axis=0)


def attend_away(queries, keys, values, lengths):
    rows, features = queries.shape[0], queries.shape[1] // 2
    positions, kv_features = keys.shape[1], keys.shape[2] // 2
    block = 16
    steps = rows // block
    hbm = pl.BlockSpec(memory_space=pltpu.HBM)
    pieces = [
        (steps, block, features),
        (steps, block, positions, kv_features),
        (steps, block, positions, kv_features),
    ]
    return pl.pallas_call(
        functools.partial(attend_away_body, features // kv_features),
        in_specs=[hbm] * 4,
        out_specs=[vmem_spec] * 5,
        out_shape=[
            jax.ShapeDtypeStruct((rows, features), jnp.float32),
            jax.ShapeDtypeStruct((rows, LANES), jnp.float32),
        ]
        + [jax.ShapeDtypeStruct(shape, jnp.bfloat16) for shape in pieces],
        scratch_shapes=[pltpu.VMEM(shape, jnp.bfloat16) for shape in pieces]
        + [
            pltpu.SMEM((rows,), jnp.int32),
            pltpu.SemaphoreType.DMA((6, steps)),
            pltpu.SemaphoreType.DMA,
        ],
        compiler_params=pltpu.CompilerParams(vmem_limit_bytes=16 * MIB),
        cost_estimate=light,
        name="attend_away",
    )(
        *(
            pltpu.with_memory_space_constraint(a, pltpu.HBM)
            for a in (lengths, queries, keys, values)
        )
    )


def attend_own(queries, keys, values, lengths):
    steps, block, features = queries.shape
    group = features // keys.shape[3]
    return pl.pallas_call(
        functools.partial(attend_own_body, group),
        in_specs=[pl.BlockSpec(memory_space=pltpu.SMEM)] + [vmem_spec] * 3,
        out_specs=[vmem_spec] * 2,
        out_shape=[
            jax.ShapeDtypeStruct((steps * block, features), jnp.float32),
            jax.ShapeDtypeStruct((steps * block, LANES), jnp.float32),
        ],
        compiler_params=pltpu.CompilerParams(vmem_limit_bytes=12 * MIB),
        cost_estimate=light,
        name="attend_own",
    )(lengths, queries, keys, values)


def places(ids, target, owned_count):
    rows = ids.shape[0]
    member = ids - target * owned_count
    owned = (member >= 0) & (member < owned_count)
    mark = jnp.where(owned, 1.0, 0.0)
    earlier = lax.broadcasted_iota(jnp.int32, (rows, rows), 1) < lax.broadcasted_iota(
        jnp.int32, (rows, rows), 0
    )
    before = jnp.dot(
        jnp.where(earlier, 1.0, 0.0).astype(jnp.bfloat16),
        mark.astype(jnp.bfloat16),
        preferred_element_type=jnp.float32,
    )
    count = jnp.sum(mark, axis=0, keepdims=True)
    row = lax.broadcasted_iota(jnp.int32, ids.shape, 0).astype(jnp.float32)
    return jnp.where(owned, before, count + row - before)


def merge_body(shifts, owned_count, own_ref, own_level, other_ref, other_level, ids_ref, out_ref, *fronts):
    rows = own_ref.shape[0]
    share = 1.0 / (1.0 + jnp.exp2(own_level[...] - other_level[...]))
    for j in range(own_ref.shape[1] // HD):
        at = slice(j * HD, (j + 1) * HD)
        own = own_ref[:, at]
        other = other_ref[:, at].astype(jnp.float32)
        out_ref[:, at] = (own + (other - own) * share[:, j : j + 1]).astype(out_ref.dtype)
    for shift, ref in zip(shifts, fronts):
        route_to(shift, owned_count, ids_ref, out_ref, ref, 0)


def route_to(shift, owned_count, ids_ref, rows_ref, out_ref, first):
    rows, slots = rows_ref.shape[0], out_ref.shape[0]
    me = lax.axis_index("adapter")
    ids = ids_ref[pl.ds(pl.multiple_of(me * rows, 16), rows), :]
    place = places(ids, lax.bitwise_xor(me, shift), owned_count).T
    slot = lax.broadcasted_iota(jnp.int32, (slots, rows), 0) + first
    take = jnp.where(place[:slots, :] == slot.astype(jnp.float32), 1.0, 0.0)
    out_ref[...] = jnp.dot(
        take.astype(jnp.bfloat16), rows_ref[...], preferred_element_type=jnp.float32
    ).astype(out_ref.dtype)


def merge(own, own_level, other, other_level, ids, owned_count, shifts, capacity):
    shapes = [own.shape] + [(capacity, own.shape[1])] * len(shifts)
    return pl.pallas_call(
        functools.partial(merge_body, shifts, owned_count),
        in_specs=[vmem_spec] * 5,
        out_specs=[vmem_spec] * len(shapes),
        out_shape=[jax.ShapeDtypeStruct(s, jnp.bfloat16) for s in shapes],
        compiler_params=pltpu.CompilerParams(vmem_limit_bytes=10 * MIB),
        cost_estimate=light,
        name="merge",
    )(own, own_level, other, other_level, ids)


def route_rest_body(first, shifts, owned_count, ids_ref, rows_ref, _, *outs):
    for shift, ref in zip(shifts, outs):
        route_to(shift, owned_count, ids_ref, rows_ref, ref, first)


def route_rest(ids, rows, after, first, owned_count, shifts):
    shape = (rows.shape[0] - first, rows.shape[1])
    return pl.pallas_call(
        functools.partial(route_rest_body, first, shifts, owned_count),
        in_specs=[vmem_spec] * 2 + [pl.BlockSpec(memory_space=pl.ANY)],
        out_specs=[vmem_spec] * len(shifts),
        out_shape=[jax.ShapeDtypeStruct(shape, jnp.bfloat16)] * len(shifts),
        compiler_params=pltpu.CompilerParams(vmem_limit_bytes=6 * MIB),
        cost_estimate=light,
        name="route_rest",
    )(ids, rows, after)


def put_back(ids, source, part, first, owned_count):
    rows, slots = ids.shape[0], part.shape[0]
    me = lax.axis_index("adapter")
    place = places(ids, me, owned_count)
    slot = lax.broadcasted_iota(jnp.int32, (rows, slots), 1) + first
    put = jnp.where(place[:, :slots] == slot.astype(jnp.float32), 1.0, 0.0)
    return jnp.dot(put.astype(jnp.bfloat16), part, preferred_element_type=jnp.float32)


def join_body(count, *refs):
    for j, ref in enumerate(refs[:count]):
        refs[-1][j] = ref[...]


def join(parts, after=()):
    shape = (len(parts), *parts[0].shape)
    return pl.pallas_call(
        functools.partial(join_body, len(parts)),
        in_specs=[vmem_spec] * len(parts) + [pl.BlockSpec(memory_space=pl.ANY)] * len(after),
        out_specs=vmem_spec,
        out_shape=jax.ShapeDtypeStruct(shape, parts[0].dtype),
        compiler_params=pltpu.CompilerParams(vmem_limit_bytes=4 * MIB),
        cost_estimate=pl.CostEstimate(flops=1000, bytes_accessed=1000, transcendentals=0),
        name="join",
    )(*parts, *after)


def restore_body(shifts, owned_count, ids_ref, *refs):
    count, outs = len(shifts), refs[-2:]
    rows = outs[0].shape[0] // count
    slots = refs[0].shape[1]
    for j, shift in enumerate(shifts):
        source = lax.bitwise_xor(lax.axis_index("adapter"), shift)
        ids = ids_ref[pl.ds(pl.multiple_of(source * rows, 16), rows), :]
        for n, out_ref in enumerate(outs):
            front = put_back(ids, source, refs[2 * n][j], 0, owned_count)
            back = put_back(ids, source, refs[2 * n + 1][j], slots, owned_count)
            out_ref[j * rows : (j + 1) * rows, :] = (front + back).astype(out_ref.dtype)


def restore(ids, own, other, after, owned_count, shifts):
    count = len(shifts)
    rows, features = own[0].shape[1] + own[1].shape[1], own[0].shape[2]
    return pl.pallas_call(
        functools.partial(restore_body, shifts, owned_count),
        in_specs=[vmem_spec] * 5 + [pl.BlockSpec(memory_space=pl.ANY)],
        out_specs=[vmem_spec] * 2,
        out_shape=[jax.ShapeDtypeStruct((count * rows, features), jnp.bfloat16)] * 2,
        compiler_params=pltpu.CompilerParams(vmem_limit_bytes=8 * MIB),
        cost_estimate=light,
        name="restore",
    )(ids, *own, *other, after)


def down_body(count, plain, rank, owned_count, ids_ref, own_ref, *refs):
    xs, (out_ref, picked_ref) = refs[:count], refs[-2:]
    me = lax.axis_index("adapter")
    rows = out_ref.shape[0] * 2 // count
    width = own_ref.shape[0]
    transposed = (((1,), (1,)), ((), ()))
    x = jnp.concatenate([r[...] for r in xs], axis=0) if count > 1 else xs[0][...]
    product = lax.dot_general(x, own_ref[...], transposed, preferred_element_type=jnp.float32)
    per_tile = LANES // rank
    first = 0
    for j in range(count):
        source = lax.bitwise_xor(me, j) if count > 1 else 0
        at = pl.ds(pl.multiple_of(source * rows, 16), rows)
        ids = ids_ref[at, :]
        member = ids - me * owned_count
        slots = xs[j].shape[0]
        if j >= plain:
            place = places(ids, me, owned_count)
            slot = lax.broadcasted_iota(jnp.int32, (slots, rows), 0).astype(jnp.float32)
            take = jnp.where(place.T[:slots, :] == slot, 1.0, 0.0).astype(jnp.bfloat16)
            member = jnp.dot(
                take,
                member.astype(jnp.float32).astype(jnp.bfloat16),
                preferred_element_type=jnp.float32,
            ).astype(jnp.int32)
        lane = lax.broadcasted_iota(jnp.int32, (slots, LANES), 1)
        picked = jnp.zeros((slots, LANES), jnp.float32)
        for t in range(width // LANES):
            part = product[first : first + slots, t * LANES : (t + 1) * LANES]
            picked += jnp.where(member == t * per_tile + lane // rank, part, 0.0)
        first += slots
        if j >= plain:
            slot = lax.broadcasted_iota(jnp.int32, (rows, slots), 1).astype(jnp.float32)
            put = jnp.where(place[:, :slots] == slot, 1.0, 0.0)
            picked = jnp.dot(
                put, picked, precision=lax.Precision.HIGHEST, preferred_element_type=jnp.float32
            )
        picked_ref[at, :] = picked + pltpu.roll(picked, rank, 1)
    packed = out_ref.shape[0]
    left = lax.broadcasted_iota(jnp.int32, (packed, LANES), 1) < rank
    out_ref[...] = jnp.where(left, picked_ref[:packed, :], picked_ref[packed:, :])


def down(ids, weight, owned_count, rank, own, plain, after=()):
    count, rows = len(own), ids.shape[0]
    return pl.pallas_call(
        functools.partial(down_body, count, plain, rank, owned_count),
        in_specs=[vmem_spec] * (2 + count) + [pl.BlockSpec(memory_space=pl.ANY)] * len(after),
        out_specs=vmem_spec,
        out_shape=jax.ShapeDtypeStruct((rows // 2, LANES), jnp.float32),
        scratch_shapes=[pltpu.VMEM((rows, LANES), jnp.float32)],
        compiler_params=pltpu.CompilerParams(vmem_limit_bytes=16 * MIB),
        cost_estimate=light,
        name="down",
    )(ids, weight, *own, *after)


def up_body(count, rank, which, with_residual, ids_ref, base_ref, up_ref, *refs):
    mids, out_ref = refs[:count], refs[-1]
    side = lax.axis_index("mp")
    packed = mids[0][...].astype(jnp.float32)
    for r in mids[1:]:
        packed += r[...].astype(jnp.float32)
    packed = packed.astype(jnp.bfloat16).astype(jnp.float32)
    turned = pltpu.roll(packed, rank, 1)
    rows = out_ref.shape[0]
    left = lax.broadcasted_iota(jnp.int32, packed.shape, 1) < rank
    if which == "all":
        at = pl.ds(0, rows)
        total = jnp.concatenate(
            [jnp.where(left, packed, turned), jnp.where(left, turned, packed)], axis=0
        )
    else:
        part = side if which == "mine" else 1 - side
        at = pl.ds(pl.multiple_of(part * rows, 16), rows)
        total = jnp.where(left == (part == 0), packed, turned)
    lane = lax.broadcasted_iota(jnp.int32, (rows, LANES), 1)
    per_tile = LANES // rank
    local = ids_ref[at, :] - side * (up_ref.shape[0] // rank)
    spread = jnp.concatenate(
        [
            jnp.where(local == t * per_tile + lane // rank, total, 0.0)
            for t in range(up_ref.shape[0] // LANES)
        ],
        axis=1,
    ).astype(jnp.bfloat16)
    delta = jnp.dot(spread, up_ref[...], preferred_element_type=jnp.float32)
    out = base_ref[at, :] + adapter_scale * delta
    if with_residual:
        out += refs[count][...].astype(jnp.float32)
    out_ref[...] = out.astype(out_ref.dtype)


def up(ids, base, weight, mids, which, rows, residual, out_type):
    rank = weight.shape[1]
    flat = weight.reshape(-1, weight.shape[2])
    extra = [] if residual is None else [residual]
    return pl.pallas_call(
        functools.partial(up_body, len(mids), rank, which, residual is not None),
        in_specs=[vmem_spec] * (3 + len(mids) + len(extra)),
        out_specs=vmem_spec,
        out_shape=jax.ShapeDtypeStruct((rows, base.shape[1]), out_type),
        compiler_params=pltpu.CompilerParams(
            vmem_limit_bytes=(24 if which == "all" else 10) * MIB
        ),
        cost_estimate=light,
        name="up",
    )(ids, base, flat, *mids, *extra)


def last_body(kept_ref, back_ref, out_ref):
    out_ref[...] = (kept_ref[...] + back_ref[...].astype(jnp.float32)).astype(out_ref.dtype)


def last(kept, back):
    return pl.pallas_call(
        last_body,
        in_specs=[vmem_spec] * 2,
        out_specs=vmem_spec,
        out_shape=jax.ShapeDtypeStruct(kept.shape, jnp.bfloat16),
        compiler_params=pltpu.CompilerParams(vmem_limit_bytes=4 * MIB),
        name="last",
    )(kept, back)


def base_body(count, unit, tile, w_ref, *refs):
    xs, ys, out_ref = refs[:count], refs[count : 2 * count], refs[-1]
    me, half = lax.axis_index("adapter"), lax.axis_index("kv")
    depth = xs[0].shape[1]
    x = jnp.concatenate([r[...] for r in xs], axis=0) if count > 1 else xs[0][...]
    y = jnp.concatenate([r[...] for r in ys], axis=0) if count > 1 else ys[0][...]
    own = pl.ds(pl.multiple_of(half * depth, depth), depth)
    other = pl.ds(pl.multiple_of((1 - half) * depth, depth), depth)
    for t in range(out_ref.shape[1] // tile):
        at = slice(t * tile, (t + 1) * tile)
        out = jnp.dot(x, w_ref[own, at], preferred_element_type=jnp.float32)
        out += jnp.dot(y, w_ref[other, at], preferred_element_type=jnp.float32)
        for j in range(out.shape[0] // unit):
            source = lax.bitwise_xor(me, j) if count > 1 else 0
            block = pl.ds(pl.multiple_of(source * unit, 16), unit)
            out_ref[block, at] = out[j * unit : (j + 1) * unit]


def base_projection(weight, own, other):
    count = len(own)
    rows = sum(b.shape[0] for b in own)
    columns = weight.shape[1]
    unit = own[0].shape[0]
    return pl.pallas_call(
        functools.partial(base_body, count, unit, min(256, columns)),
        in_specs=[vmem_spec] * (1 + 2 * count),
        out_specs=vmem_spec,
        out_shape=jax.ShapeDtypeStruct((rows, columns), jnp.float32),
        compiler_params=pltpu.CompilerParams(vmem_limit_bytes=24 * MIB),
        cost_estimate=light,
        name="base",
    )(weight, *own, *other)


def swapped(x, axis, other=1):
    return lax.ppermute(x, axis, [(i, i ^ other) for i in range(lax.axis_size(axis))])


def local(
    queries,
    keys,
    values,
    lengths,
    row_adapter_index,
    residual,
    output_weight,
    adapter_down_weight,
    adapter_up_weight,
):
    owners, splits = lax.axis_size("adapter"), lax.axis_size("mp")
    entire_rows = row_adapter_index.shape[0]
    kept_rows = entire_rows // splits
    direct = owners == 4 and splits == 2
    owned_count = adapter_down_weight.shape[0]
    capacity = 2 * queries.shape[0] // owners
    ids = jnp.broadcast_to(row_adapter_index[:, None], (entire_rows, LANES))

    sent, sent_level, *own_operands = attend_away(queries, keys, values, lengths)
    got, got_level = swapped(sent, "kv"), swapped(sent_level, "kv")
    own, own_level = attend_own(*own_operands, lengths)
    shifts = tuple(range(2, owners)) if direct else ()
    attended, *fronts = merge(
        own, own_level, got, got_level, ids, owned_count, shifts, capacity
    )

    rank = adapter_down_weight.shape[2]
    down_own = jnp.transpose(adapter_down_weight, (0, 2, 1)).reshape(-1, attended.shape[1])
    if direct:
        fronts = [swapped(f, "adapter", j) for j, f in zip(shifts, fronts)]
        beside = swapped(attended, "adapter", 1)
        own = [attended, beside]
        other = [swapped(b, "kv") for b in own]
        backs = route_rest(ids, attended, fronts[0], capacity, owned_count, shifts)
        part = down(ids, down_own, owned_count, rank, own + fronts, 2, [backs[0], other[0]])
        backs = [swapped(b, "adapter", j) for j, b in zip(shifts, backs)]
        routed = [join(fronts), join(backs, ())]
        part = part + swapped(part, "mp")
        part = (part + swapped(part, "kv")).astype(jnp.bfloat16)
        mids = [part] + [swapped(part, "adapter", j) for j in range(owners - 1, 0, -1)]
        own_rest, other_rest = restore(
            ids, routed, [swapped(r, "kv") for r in routed], part, owned_count, shifts
        )
        base = base_projection(output_weight, own + [own_rest], other + [other_rest])
        away = up(
            ids, base, adapter_up_weight, mids, "theirs", kept_rows, None, jnp.bfloat16
        )
        back = swapped(away, "mp")
        kept = up(
            ids, base, adapter_up_weight, mids, "mine", kept_rows, residual, jnp.float32
        )
        return last(kept, back)
    blocks = lax.all_gather(attended, "adapter", axis=0, tiled=True)
    others = swapped(blocks, "kv")
    part = down(ids, down_own, owned_count, rank, [blocks], 1)
    mids = [lax.psum(part, ("adapter", "mp", "kv"))]
    base = base_projection(output_weight, [blocks], [others])
    terms = up(ids, base, adapter_up_weight, mids, "all", entire_rows, None, jnp.float32)
    summed = lax.psum_scatter(terms, "mp", scatter_dimension=0, tiled=True)
    return (residual.astype(jnp.float32) + summed).astype(jnp.bfloat16)


def solution(mesh):
    placed = (
        P(("groups", "adapter"), "mp"),
        P(("groups", "adapter"), "kv", "mp"),
        P(("groups", "adapter"), "kv", "mp"),
        P(("groups", "adapter")),
        P("groups"),
        P(("groups", "mp"), ("adapter", "kv")),
        P("mp", ("adapter", "kv")),
        P("adapter", ("mp", "kv"), None),
        P("mp", None, ("adapter", "kv")),
    )
    return jax.shard_map(
        local,
        mesh=mesh,
        in_specs=placed,
        out_specs=P(("groups", "mp"), ("adapter", "kv")),
        check_vma=False,
    )
```

```python
import functools
import math

import jax
import jax.numpy as jnp
from jax import lax
from jax.experimental import pallas as pl
from jax.experimental.pallas import tpu as pltpu
from jax.sharding import PartitionSpec as P

HD = 128
LANES = 128
MIB = 1 << 20

neg_big = -1e30
adapter_scale = 2.0
score_scale = 1.0 / math.sqrt(HD)
log2_e = 1.4426950408889634


vmem_spec = pl.BlockSpec(memory_space=pltpu.VMEM)
light = pl.CostEstimate(flops=1000, bytes_accessed=1000, transcendentals=0)


def attend_away_body(group, lengths_hbm, q_hbm, k_hbm, v_hbm, o_ref, s_ref, *refs):
    own, fetched, (lengths, sems, sem) = refs[:3], refs[3:6], refs[6:]
    core = lax.axis_index("kv")
    steps, rows = own[0].shape[:2]

    def copies(half, dst, first, i):
        at = pl.ds(i * rows, rows)
        for n, (hbm, ref) in enumerate(zip((q_hbm, k_hbm, v_hbm), dst)):
            width = ref.shape[-1]
            columns = pl.ds(pl.multiple_of(half * width, width), width)
            src = hbm.at[at, columns] if n == 0 else hbm.at[at, :, columns]
            yield pltpu.make_async_copy(src, ref.at[i], sems.at[first + n, i])

    number = pltpu.make_async_copy(lengths_hbm, lengths, sem)
    number.start()
    for half, dst, first in ((1 - core, fetched, 0), (core, own, 3)):
        for i in range(steps):
            for copy in copies(half, dst, first, i):
                copy.start()
    number.wait()
    for i in range(steps):
        for copy in copies(1 - core, fetched, 0, i):
            copy.wait()
        attend_block(group, core, i, lengths, *fetched, o_ref, s_ref)
    for i in range(steps):
        for copy in copies(core, own, 3, i):
            copy.wait()


def attend_own_body(group, lengths, q_ref, k_ref, v_ref, o_ref, s_ref):
    for i in range(q_ref.shape[0]):
        attend_block(group, lax.axis_index("kv"), i, lengths, q_ref, k_ref, v_ref, o_ref, s_ref)


def attend_block(group, core, i, lengths, q_ref, k_ref, v_ref, o_ref, s_ref):
    positions = k_ref.shape[2]
    rows, kv_heads = q_ref.shape[1], k_ref.shape[3] // HD
    offset = core * positions
    wide = 8 * positions
    row_id = lax.broadcasted_iota(jnp.int32, (8, wide), 0)
    column = lax.broadcasted_iota(jnp.int32, (8, wide), 1)
    own_row = column // positions == row_id
    position = column % positions + offset
    lane = lax.broadcasted_iota(jnp.int32, (8, LANES), 1)
    ones = jnp.ones((wide, LANES), jnp.bfloat16)
    queries = q_ref[i].astype(jnp.float32)
    outs = {}
    stats = []
    for sub in range(rows // 8):
        limit = jnp.zeros((8, wide), jnp.int32)
        for t in range(8):
            limit = jnp.where(row_id == t, lengths[i * rows + sub * 8 + t], limit)
        valid = own_row & (position < limit)
        stat = jnp.zeros((8, LANES), jnp.float32)
        for g in range(kv_heads):
            q = jnp.concatenate(
                [
                    queries[sub * 8 : sub * 8 + 8, j * HD : (j + 1) * HD]
                    for j in range(g * group, (g + 1) * group)
                ],
                axis=0,
            ).astype(jnp.bfloat16)
            k = k_ref[i, sub * 8 : sub * 8 + 8, :, g * HD : (g + 1) * HD].reshape(wide, HD)
            v = v_ref[i, sub * 8 : sub * 8 + 8, :, g * HD : (g + 1) * HD].reshape(wide, HD)
            scores = lax.dot_general(
                q, k, (((1,), (1,)), ((), ())), preferred_element_type=jnp.float32
            ).reshape(group, 8, wide)
            scores = jnp.where(valid[None], scores, neg_big)
            top = jnp.max(scores, axis=2, keepdims=True)
            weights = jnp.exp2((scores - top) * (score_scale * log2_e))
            weights = weights.astype(jnp.bfloat16).reshape(group * 8, wide)
            both = jnp.dot(
                weights,
                jnp.concatenate([v, ones], axis=1),
                preferred_element_type=jnp.float32,
            )
            total = both[:, HD:]
            out = both[:, :HD] / total
            level = jnp.log2(total) + top.reshape(group * 8, 1) * (score_scale * log2_e)
            for j in range(group):
                outs[sub, g * group + j] = out[j * 8 : j * 8 + 8]
                stat = jnp.where(lane == g * group + j, level[j * 8 : j * 8 + 8], stat)
        stats.append(stat)
    at = slice(i * rows, (i + 1) * rows)
    for j in range(kv_heads * group):
        o_ref[at, j * HD : (j + 1) * HD] = jnp.concatenate(
            [outs[sub, j] for sub in range(rows // 8)], axis=0
        ).astype(o_ref.dtype)
    s_ref[at, :] = jnp.concatenate(stats, axis=0)


def attend_away(queries, keys, values, lengths):
    rows, features = queries.shape[0], queries.shape[1] // 2
    positions, kv_features = keys.shape[1], keys.shape[2] // 2
    block = 16
    steps = rows // block
    hbm = pl.BlockSpec(memory_space=pltpu.HBM)
    pieces = [
        (steps, block, features),
        (steps, block, positions, kv_features),
        (steps, block, positions, kv_features),
    ]
    return pl.pallas_call(
        functools.partial(attend_away_body, features // kv_features),
        in_specs=[hbm] * 4,
        out_specs=[vmem_spec] * 5,
        out_shape=[
            jax.ShapeDtypeStruct((rows, features), jnp.float32),
            jax.ShapeDtypeStruct((rows, LANES), jnp.float32),
        ]
        + [jax.ShapeDtypeStruct(shape, jnp.bfloat16) for shape in pieces],
        scratch_shapes=[pltpu.VMEM(shape, jnp.bfloat16) for shape in pieces]
        + [
            pltpu.SMEM((rows,), jnp.int32),
            pltpu.SemaphoreType.DMA((6, steps)),
            pltpu.SemaphoreType.DMA,
        ],
        compiler_params=pltpu.CompilerParams(vmem_limit_bytes=16 * MIB),
        cost_estimate=light,
        name="attend_away",
    )(
        *(
            pltpu.with_memory_space_constraint(a, pltpu.HBM)
            for a in (lengths, queries, keys, values)
        )
    )


def attend_own(queries, keys, values, lengths):
    steps, block, features = queries.shape
    group = features // keys.shape[3]
    return pl.pallas_call(
        functools.partial(attend_own_body, group),
        in_specs=[pl.BlockSpec(memory_space=pltpu.SMEM)] + [vmem_spec] * 3,
        out_specs=[vmem_spec] * 2,
        out_shape=[
            jax.ShapeDtypeStruct((steps * block, features), jnp.float32),
            jax.ShapeDtypeStruct((steps * block, LANES), jnp.float32),
        ],
        compiler_params=pltpu.CompilerParams(vmem_limit_bytes=12 * MIB),
        cost_estimate=light,
        name="attend_own",
    )(lengths, queries, keys, values)


def places(ids, target, owned_count):
    rows = ids.shape[0]
    member = ids - target * owned_count
    owned = (member >= 0) & (member < owned_count)
    mark = jnp.where(owned, 1.0, 0.0)
    earlier = lax.broadcasted_iota(jnp.int32, (rows, rows), 1) < lax.broadcasted_iota(
        jnp.int32, (rows, rows), 0
    )
    before = jnp.dot(
        jnp.where(earlier, 1.0, 0.0).astype(jnp.bfloat16),
        mark.astype(jnp.bfloat16),
        preferred_element_type=jnp.float32,
    )
    count = jnp.sum(mark, axis=0, keepdims=True)
    row = lax.broadcasted_iota(jnp.int32, ids.shape, 0).astype(jnp.float32)
    return jnp.where(owned, before, count + row - before)


def merge_body(shifts, owned_count, own_ref, own_level, other_ref, other_level, ids_ref, out_ref, *fronts):
    rows = own_ref.shape[0]
    share = 1.0 / (1.0 + jnp.exp2(own_level[...] - other_level[...]))
    for j in range(own_ref.shape[1] // HD):
        at = slice(j * HD, (j + 1) * HD)
        own = own_ref[:, at]
        other = other_ref[:, at].astype(jnp.float32)
        out_ref[:, at] = (own + (other - own) * share[:, j : j + 1]).astype(out_ref.dtype)
    for shift, ref in zip(shifts, fronts):
        route_to(shift, owned_count, ids_ref, out_ref, ref, 0)


def route_to(shift, owned_count, ids_ref, rows_ref, out_ref, first):
    rows, slots = rows_ref.shape[0], out_ref.shape[0]
    me = lax.axis_index("adapter")
    ids = ids_ref[pl.ds(pl.multiple_of(me * rows, 16), rows), :]
    place = places(ids, lax.bitwise_xor(me, shift), owned_count).T
    slot = lax.broadcasted_iota(jnp.int32, (slots, rows), 0) + first
    take = jnp.where(place[:slots, :] == slot.astype(jnp.float32), 1.0, 0.0)
    out_ref[...] = jnp.dot(
        take.astype(jnp.bfloat16), rows_ref[...], preferred_element_type=jnp.float32
    ).astype(out_ref.dtype)


def merge(own, own_level, other, other_level, ids, owned_count, shifts, capacity):
    shapes = [own.shape] + [(capacity, own.shape[1])] * len(shifts)
    return pl.pallas_call(
        functools.partial(merge_body, shifts, owned_count),
        in_specs=[vmem_spec] * 5,
        out_specs=[vmem_spec] * len(shapes),
        out_shape=[jax.ShapeDtypeStruct(s, jnp.bfloat16) for s in shapes],
        compiler_params=pltpu.CompilerParams(vmem_limit_bytes=10 * MIB),
        cost_estimate=light,
        name="merge",
    )(own, own_level, other, other_level, ids)


def route_rest_body(first, shifts, owned_count, ids_ref, rows_ref, _, *outs):
    for shift, ref in zip(shifts, outs):
        route_to(shift, owned_count, ids_ref, rows_ref, ref, first)


def route_rest(ids, rows, after, first, owned_count, shifts):
    shape = (rows.shape[0] - first, rows.shape[1])
    return pl.pallas_call(
        functools.partial(route_rest_body, first, shifts, owned_count),
        in_specs=[vmem_spec] * 2 + [pl.BlockSpec(memory_space=pl.ANY)],
        out_specs=[vmem_spec] * len(shifts),
        out_shape=[jax.ShapeDtypeStruct(shape, jnp.bfloat16)] * len(shifts),
        compiler_params=pltpu.CompilerParams(vmem_limit_bytes=6 * MIB),
        cost_estimate=light,
        name="route_rest",
    )(ids, rows, after)


def put_back(ids, source, part, first, owned_count):
    rows, slots = ids.shape[0], part.shape[0]
    me = lax.axis_index("adapter")
    place = places(ids, me, owned_count)
    slot = lax.broadcasted_iota(jnp.int32, (rows, slots), 1) + first
    put = jnp.where(place[:, :slots] == slot.astype(jnp.float32), 1.0, 0.0)
    return jnp.dot(put.astype(jnp.bfloat16), part, preferred_element_type=jnp.float32)


def join_body(count, *refs):
    for j, ref in enumerate(refs[:count]):
        refs[-1][j] = ref[...]


def join(parts, after=()):
    shape = (len(parts), *parts[0].shape)
    return pl.pallas_call(
        functools.partial(join_body, len(parts)),
        in_specs=[vmem_spec] * len(parts) + [pl.BlockSpec(memory_space=pl.ANY)] * len(after),
        out_specs=vmem_spec,
        out_shape=jax.ShapeDtypeStruct(shape, parts[0].dtype),
        compiler_params=pltpu.CompilerParams(vmem_limit_bytes=4 * MIB),
        cost_estimate=pl.CostEstimate(flops=1000, bytes_accessed=1000, transcendentals=0),
        name="join",
    )(*parts, *after)


def restore_body(shifts, owned_count, ids_ref, *refs):
    count, outs = len(shifts), refs[-2:]
    rows = outs[0].shape[0] // count
    slots = refs[0].shape[1]
    for j, shift in enumerate(shifts):
        source = lax.bitwise_xor(lax.axis_index("adapter"), shift)
        ids = ids_ref[pl.ds(pl.multiple_of(source * rows, 16), rows), :]
        for n, out_ref in enumerate(outs):
            front = put_back(ids, source, refs[2 * n][j], 0, owned_count)
            back = put_back(ids, source, refs[2 * n + 1][j], slots, owned_count)
            out_ref[j * rows : (j + 1) * rows, :] = (front + back).astype(out_ref.dtype)


def restore(ids, own, other, after, owned_count, shifts):
    count = len(shifts)
    rows, features = own[0].shape[1] + own[1].shape[1], own[0].shape[2]
    return pl.pallas_call(
        functools.partial(restore_body, shifts, owned_count),
        in_specs=[vmem_spec] * 5 + [pl.BlockSpec(memory_space=pl.ANY)],
        out_specs=[vmem_spec] * 2,
        out_shape=[jax.ShapeDtypeStruct((count * rows, features), jnp.bfloat16)] * 2,
        compiler_params=pltpu.CompilerParams(vmem_limit_bytes=8 * MIB),
        cost_estimate=light,
        name="restore",
    )(ids, *own, *other, after)


def down_body(count, plain, rank, owned_count, ids_ref, own_ref, *refs):
    xs, (out_ref, picked_ref) = refs[:count], refs[-2:]
    me = lax.axis_index("adapter")
    rows = out_ref.shape[0] * 2 // count
    width = own_ref.shape[0]
    transposed = (((1,), (1,)), ((), ()))
    x = jnp.concatenate([r[...] for r in xs], axis=0) if count > 1 else xs[0][...]
    product = lax.dot_general(x, own_ref[...], transposed, preferred_element_type=jnp.float32)
    per_tile = LANES // rank
    first = 0
    for j in range(count):
        source = lax.bitwise_xor(me, j) if count > 1 else 0
        at = pl.ds(pl.multiple_of(source * rows, 16), rows)
        ids = ids_ref[at, :]
        member = ids - me * owned_count
        slots = xs[j].shape[0]
        if j >= plain:
            place = places(ids, me, owned_count)
            slot = lax.broadcasted_iota(jnp.int32, (slots, rows), 0).astype(jnp.float32)
            take = jnp.where(place.T[:slots, :] == slot, 1.0, 0.0).astype(jnp.bfloat16)
            member = jnp.dot(
                take,
                member.astype(jnp.float32).astype(jnp.bfloat16),
                preferred_element_type=jnp.float32,
            ).astype(jnp.int32)
        lane = lax.broadcasted_iota(jnp.int32, (slots, LANES), 1)
        picked = jnp.zeros((slots, LANES), jnp.float32)
        for t in range(width // LANES):
            part = product[first : first + slots, t * LANES : (t + 1) * LANES]
            picked += jnp.where(member == t * per_tile + lane // rank, part, 0.0)
        first += slots
        if j >= plain:
            slot = lax.broadcasted_iota(jnp.int32, (rows, slots), 1).astype(jnp.float32)
            put = jnp.where(place[:, :slots] == slot, 1.0, 0.0)
            picked = jnp.dot(
                put, picked, precision=lax.Precision.HIGHEST, preferred_element_type=jnp.float32
            )
        picked_ref[at, :] = picked + pltpu.roll(picked, rank, 1)
    packed = out_ref.shape[0]
    left = lax.broadcasted_iota(jnp.int32, (packed, LANES), 1) < rank
    out_ref[...] = jnp.where(left, picked_ref[:packed, :], picked_ref[packed:, :])


def down(ids, weight, owned_count, rank, own, plain, after=()):
    count, rows = len(own), ids.shape[0]
    return pl.pallas_call(
        functools.partial(down_body, count, plain, rank, owned_count),
        in_specs=[vmem_spec] * (2 + count) + [pl.BlockSpec(memory_space=pl.ANY)] * len(after),
        out_specs=vmem_spec,
        out_shape=jax.ShapeDtypeStruct((rows // 2, LANES), jnp.float32),
        scratch_shapes=[pltpu.VMEM((rows, LANES), jnp.float32)],
        compiler_params=pltpu.CompilerParams(vmem_limit_bytes=16 * MIB),
        cost_estimate=light,
        name="down",
    )(ids, weight, *own, *after)


def up_body(count, rank, which, with_residual, ids_ref, base_ref, up_ref, *refs):
    mids, out_ref = refs[:count], refs[-1]
    side = lax.axis_index("mp")
    packed = mids[0][...].astype(jnp.float32)
    for r in mids[1:]:
        packed += r[...].astype(jnp.float32)
    packed = packed.astype(jnp.bfloat16).astype(jnp.float32)
    turned = pltpu.roll(packed, rank, 1)
    rows = out_ref.shape[0]
    left = lax.broadcasted_iota(jnp.int32, packed.shape, 1) < rank
    if which == "all":
        at = pl.ds(0, rows)
        total = jnp.concatenate(
            [jnp.where(left, packed, turned), jnp.where(left, turned, packed)], axis=0
        )
    else:
        part = side if which == "mine" else 1 - side
        at = pl.ds(pl.multiple_of(part * rows, 16), rows)
        total = jnp.where(left == (part == 0), packed, turned)
    lane = lax.broadcasted_iota(jnp.int32, (rows, LANES), 1)
    per_tile = LANES // rank
    local = ids_ref[at, :] - side * (up_ref.shape[0] // rank)
    spread = jnp.concatenate(
        [
            jnp.where(local == t * per_tile + lane // rank, total, 0.0)
            for t in range(up_ref.shape[0] // LANES)
        ],
        axis=1,
    ).astype(jnp.bfloat16)
    delta = jnp.dot(spread, up_ref[...], preferred_element_type=jnp.float32)
    out = base_ref[at, :] + adapter_scale * delta
    if with_residual:
        out += refs[count][...].astype(jnp.float32)
    out_ref[...] = out.astype(out_ref.dtype)


def up(ids, base, weight, mids, which, rows, residual, out_type):
    rank = weight.shape[1]
    flat = weight.reshape(-1, weight.shape[2])
    extra = [] if residual is None else [residual]
    return pl.pallas_call(
        functools.partial(up_body, len(mids), rank, which, residual is not None),
        in_specs=[vmem_spec] * (3 + len(mids) + len(extra)),
        out_specs=vmem_spec,
        out_shape=jax.ShapeDtypeStruct((rows, base.shape[1]), out_type),
        compiler_params=pltpu.CompilerParams(
            vmem_limit_bytes=(24 if which == "all" else 10) * MIB
        ),
        cost_estimate=light,
        name="up",
    )(ids, base, flat, *mids, *extra)


def last_body(kept_ref, back_ref, out_ref):
    out_ref[...] = (kept_ref[...] + back_ref[...].astype(jnp.float32)).astype(out_ref.dtype)


def last(kept, back):
    return pl.pallas_call(
        last_body,
        in_specs=[vmem_spec] * 2,
        out_specs=vmem_spec,
        out_shape=jax.ShapeDtypeStruct(kept.shape, jnp.bfloat16),
        compiler_params=pltpu.CompilerParams(vmem_limit_bytes=4 * MIB),
        name="last",
    )(kept, back)


def base_body(count, unit, tile, w_ref, *refs):
    xs, ys, out_ref = refs[:count], refs[count : 2 * count], refs[-1]
    me, half = lax.axis_index("adapter"), lax.axis_index("kv")
    depth = xs[0].shape[1]
    x = jnp.concatenate([r[...] for r in xs], axis=0) if count > 1 else xs[0][...]
    y = jnp.concatenate([r[...] for r in ys], axis=0) if count > 1 else ys[0][...]
    own = pl.ds(pl.multiple_of(half * depth, depth), depth)
    other = pl.ds(pl.multiple_of((1 - half) * depth, depth), depth)
    for t in range(out_ref.shape[1] // tile):
        at = slice(t * tile, (t + 1) * tile)
        out = jnp.dot(x, w_ref[own, at], preferred_element_type=jnp.float32)
        out += jnp.dot(y, w_ref[other, at], preferred_element_type=jnp.float32)
        for j in range(out.shape[0] // unit):
            source = lax.bitwise_xor(me, j) if count > 1 else 0
            block = pl.ds(pl.multiple_of(source * unit, 16), unit)
            out_ref[block, at] = out[j * unit : (j + 1) * unit]


def base_projection(weight, own, other):
    count = len(own)
    rows = sum(b.shape[0] for b in own)
    columns = weight.shape[1]
    unit = own[0].shape[0]
    return pl.pallas_call(
        functools.partial(base_body, count, unit, min(256, columns)),
        in_specs=[vmem_spec] * (1 + 2 * count),
        out_specs=vmem_spec,
        out_shape=jax.ShapeDtypeStruct((rows, columns), jnp.float32),
        compiler_params=pltpu.CompilerParams(vmem_limit_bytes=24 * MIB),
        cost_estimate=light,
        name="base",
    )(weight, *own, *other)


def swapped(x, axis, other=1):
    return lax.ppermute(x, axis, [(i, i ^ other) for i in range(lax.axis_size(axis))])


def local(
    queries,
    keys,
    values,
    lengths,
    row_adapter_index,
    residual,
    output_weight,
    adapter_down_weight,
    adapter_up_weight,
):
    owners, splits = lax.axis_size("adapter"), lax.axis_size("mp")
    entire_rows = row_adapter_index.shape[0]
    kept_rows = entire_rows // splits
    direct = owners == 4 and splits == 2
    owned_count = adapter_down_weight.shape[0]
    capacity = 2 * queries.shape[0] // owners
    ids = jnp.broadcast_to(row_adapter_index[:, None], (entire_rows, LANES))

    sent, sent_level, *own_operands = attend_away(queries, keys, values, lengths)
    got, got_level = swapped(sent, "kv"), swapped(sent_level, "kv")
    own, own_level = attend_own(*own_operands, lengths)
    shifts = tuple(range(2, owners)) if direct else ()
    attended, *fronts = merge(
        own, own_level, got, got_level, ids, owned_count, shifts, capacity
    )

    rank = adapter_down_weight.shape[2]
    down_own = jnp.transpose(adapter_down_weight, (0, 2, 1)).reshape(-1, attended.shape[1])
    if direct:
        fronts = [swapped(f, "adapter", j) for j, f in zip(shifts, fronts)]
        beside = swapped(attended, "adapter", 1)
        own = [attended, beside]
        other = [swapped(b, "kv") for b in own]
        backs = route_rest(ids, attended, fronts[0], capacity, owned_count, shifts)
        part = down(ids, down_own, owned_count, rank, own + fronts, 2, [backs[0], other[0]])
        backs = [swapped(b, "adapter", j) for j, b in zip(shifts, backs)]
        routed = [join(fronts), join(backs, ())]
        chip = splits * lax.axis_size("kv")
        across = lax.ppermute(part, ("mp", "kv"), [(i, chip - 1 - i) for i in range(chip)])
        part = (part + swapped(part, "mp") + swapped(part, "kv") + across).astype(jnp.bfloat16)
        mids = [part] + [swapped(part, "adapter", j) for j in range(owners - 1, 0, -1)]
        own_rest, other_rest = restore(
            ids, routed, [swapped(r, "kv") for r in routed], part, owned_count, shifts
        )
        base = base_projection(output_weight, own + [own_rest], other + [other_rest])
        away = up(
            ids, base, adapter_up_weight, mids, "theirs", kept_rows, None, jnp.bfloat16
        )
        back = swapped(away, "mp")
        kept = up(
            ids, base, adapter_up_weight, mids, "mine", kept_rows, residual, jnp.float32
        )
        return last(kept, back)
    blocks = lax.all_gather(attended, "adapter", axis=0, tiled=True)
    others = swapped(blocks, "kv")
    part = down(ids, down_own, owned_count, rank, [blocks], 1)
    mids = [lax.psum(part, ("adapter", "mp", "kv"))]
    base = base_projection(output_weight, [blocks], [others])
    terms = up(ids, base, adapter_up_weight, mids, "all", entire_rows, None, jnp.float32)
    summed = lax.psum_scatter(terms, "mp", scatter_dimension=0, tiled=True)
    return (residual.astype(jnp.float32) + summed).astype(jnp.bfloat16)


def solution(mesh):
    placed = (
        P(("groups", "adapter"), "mp"),
        P(("groups", "adapter"), "kv", "mp"),
        P(("groups", "adapter"), "kv", "mp"),
        P(("groups", "adapter")),
        P("groups"),
        P(("groups", "mp"), ("adapter", "kv")),
        P("mp", ("adapter", "kv")),
        P("adapter", ("mp", "kv"), None),
        P("mp", None, ("adapter", "kv")),
    )
    return jax.shard_map(
        local,
        mesh=mesh,
        in_specs=placed,
        out_specs=P(("groups", "mp"), ("adapter", "kv")),
        check_vma=False,
    )
```
